32 devices in a mesh: trial: 2 (over core), tmpl: 16 (over z, y, x).
Axes of the slice: x: 2, y: 2, z: 4, core: 2. Of those that a mesh axis runs over, the one named last changes fastest.
Arguments:
- spectra: bfloat16 [2, 2, 16, 2, 16896], P(None, 'trial', 'tmpl'), may hold values from -6 to 6
- half_spectra: bfloat16 [2, 2, 16, 2, 8704], P(None, 'trial', 'tmpl'), may hold values from -6 to 6
- kernels: bfloat16 [256, 2, 512], P('tmpl'), may hold values from -0.1875 to 0.1875
- owners: int32 [2, 2], replicated, may hold values from 0 to 31, as said below
- counts: int32 [16], replicated, may hold values from 12 to 16, as said below
- partners: int32 [256], replicated, may hold values from -1 to 255, as said below
Outputs:
- powers: bfloat16 [2, 2, 256, 16384], P(None, 'trial', 'tmpl')
The draws below stay inside these ranges and needn't reach their ends.
Inputs may be any that keep to these rules, and one draw needn't show every extreme that they name: owners[w, t] = i * 16 + c names the device with trial index i and tmpl index c that holds window w's data of trial t; the two trials of a window lie on different trial indices, and the trial index holding trial 0 alternates from one window to the next; in some window the two trials lie on devices 0 and 31. The live templates of tmpl index d are its first counts[d]; some index has all 16 live. For a live template j, partners[j] is a live template; the live templates of one tmpl index name templates of any one tmpl index at most 1 times, and some index does so exactly 1 times; partners[j] = -1 for every template that is not live.
All inputs are finite; a program needn't handle non-finite values.
Results may differ from the reference program's by a relative error of at most 0.004.
Values may be sent and summed in bfloat16 or wider, within the bound.
A program may use at most 128 MiB of HBM per device.

```python
import jax
import jax.numpy as jnp

BINS = 16384
TAPS = 512
TMPL_DEV = 16
WINDOWS = 2
HALF_BINS = 8192
SLAB = 16896
HALF_SLAB = 8704
TEMPLATES = 256
CAPACITY = 1
N_TRIAL = 2
N_TMPL = 16


def live_counts(key):
    devices_count = TEMPLATES // TMPL_DEV
    lowest = max(1, 3 * TMPL_DEV // 4)
    drawn_counts = jax.random.randint(jax.random.fold_in(key, 101), (devices_count,), lowest, TMPL_DEV + 1)
    filled = jax.random.randint(jax.random.fold_in(key, 102), (), 0, devices_count)
    return jnp.where(jnp.arange(devices_count) == filled, TMPL_DEV, drawn_counts).astype(jnp.int32)


def draw_counts(key, part):
    return live_counts(key)


def draw_partners(key, part):
    devices_count = TEMPLATES // TMPL_DEV
    counts = live_counts(key)
    slot_total = CAPACITY * devices_count
    noise_int = jax.random.randint(jax.random.fold_in(key, 201), (devices_count, slot_total), 0, 2 ** 20)
    favour = jax.random.randint(jax.random.fold_in(key, 202), (devices_count,), 0, 2 ** 20)
    lane_ids = jnp.arange(slot_total, dtype=jnp.int32)
    scores = (noise_int + favour[lane_ids // CAPACITY][None, :]) * slot_total + lane_ids[None, :]
    ordering = jnp.argsort(-scores, axis=1, stable=True)[:, :TMPL_DEV]
    holders = (ordering // CAPACITY).astype(jnp.int32)
    within = jax.random.randint(jax.random.fold_in(key, 203), (devices_count, TMPL_DEV), 0, counts[holders])
    chosen = holders * TMPL_DEV + within
    live_mask = jnp.arange(TMPL_DEV)[None, :] < counts[:, None]
    return jnp.where(live_mask, chosen, -1).reshape(TEMPLATES).astype(jnp.int32)


def draw_owners(key, part):
    devices_count = TEMPLATES // TMPL_DEV
    phase_bit = jax.random.randint(jax.random.fold_in(key, 301), (), 0, 2)
    first_row = (jnp.arange(WINDOWS, dtype=jnp.int32) + phase_bit) % 2
    row_pick = jnp.stack([first_row, 1 - first_row], axis=1)
    columns = jax.random.randint(jax.random.fold_in(key, 302), (WINDOWS, 2), 0, devices_count)
    extreme_window = jax.random.randint(jax.random.fold_in(key, 303), (), 0, WINDOWS)
    extreme_columns = jnp.where(row_pick == 0, 0, devices_count - 1)
    is_extreme = (jnp.arange(WINDOWS, dtype=jnp.int32) == extreme_window)[:, None]
    columns = jnp.where(is_extreme, extreme_columns, columns)
    return (row_pick * devices_count + columns).astype(jnp.int32)


def level_of(rng, extent, cuts, low, largest):
    level, own = 1.0, jax.random.fold_in(rng, 6)
    for position, blocks in cuts:
        heights = jnp.exp(jax.random.uniform(jax.random.fold_in(own, position), (blocks,), jnp.float32, low / len(cuts), largest / len(cuts)))
        level = level * jnp.repeat(heights, extent[position] // blocks).reshape([-1 if axis == position else 1 for axis in range(len(extent))])
    return level


def scatter_about(rng, shape, scale, most, split=(), kind=jnp.bfloat16):
    factor_of = level_of(rng, shape, split, -0.22, 0.18) if split else 1.0
    drawn = jax.random.normal(rng, shape, jnp.float32) * scale * factor_of
    return jnp.minimum(jnp.maximum(drawn, -most), most).astype(kind)


def setup_inputs(seed: int = 0) -> dict:
    arg_keys = jax.random.split(jax.random.key(seed), 7)
    spectra = scatter_about(arg_keys[0], (WINDOWS, N_TRIAL, N_TMPL, 2, SLAB), 1.0, 6.0, ((1, 2), (2, 16)))
    half_spectra = scatter_about(arg_keys[1], (WINDOWS, N_TRIAL, N_TMPL, 2, HALF_SLAB), 1.0, 6.0, ((1, 2), (2, 16)))
    kernels = scatter_about(arg_keys[2], (TEMPLATES, 2, TAPS), (2 * TAPS) ** -0.5, 0.1875, ((0, 16),))
    owners = draw_owners(jax.random.fold_in(arg_keys[6], 71), 0)
    counts = draw_counts(jax.random.fold_in(arg_keys[6], 71), 0)
    partners = draw_partners(jax.random.fold_in(arg_keys[6], 71), 0)
    return {"spectra": spectra, "half_spectra": half_spectra, "kernels": kernels, "owners": owners, "counts": counts, "partners": partners}


def hankel_rows(signal, tap_count, columns):
    length = signal.shape[1]
    repeated = jnp.broadcast_to(signal[:, None, :], (2, tap_count + 1, length)).reshape(2, (tap_count + 1) * length)
    skewed = repeated[:, : tap_count * (length + 1)].reshape(2, tap_count, length + 1)
    return skewed[:, :, :columns].reshape(2 * tap_count, columns)


def kernel_matrix(kernel_set):
    real_part = kernel_set[:, 0, :]
    imag_part = kernel_set[:, 1, :]
    upper_rows = jnp.concatenate([real_part, -imag_part], axis=1)
    lower_rows = jnp.concatenate([imag_part, real_part], axis=1)
    return jnp.concatenate([upper_rows, lower_rows], axis=0)


def power_rows(weights, stacked):
    product = jnp.dot(weights, stacked, preferred_element_type=jnp.float32)
    middle = weights.shape[0] // 2
    return product[:middle] * product[:middle] + product[middle:] * product[middle:]


def reference(spectra, half_spectra, kernels, owners, counts, partners):
    weights = kernel_matrix(kernels)
    indices = jnp.arange(TEMPLATES, dtype=jnp.int32)
    live_mask = (indices % TMPL_DEV) < counts[indices // TMPL_DEV]
    sources = jnp.maximum(partners, 0)
    windows_out = []
    for window in range(WINDOWS):
        trials_out = []
        for trial_index in range(N_TRIAL):
            owner_id = owners[window, trial_index]
            whole_slab = spectra[window, owner_id // N_TMPL, owner_id % N_TMPL]
            halved = half_spectra[window, owner_id // N_TMPL, owner_id % N_TMPL]
            direct = power_rows(weights, hankel_rows(whole_slab, TAPS, BINS))
            planes = power_rows(weights, hankel_rows(halved, TAPS, HALF_BINS)).astype(jnp.bfloat16)
            borrowed = jnp.repeat(planes[sources], 2, axis=1).astype(jnp.float32)
            summed = jnp.where(live_mask[:, None], direct + borrowed, jnp.float32(0.0))
            trials_out.append(summed.astype(jnp.bfloat16))
        windows_out.append(jnp.stack(trials_out))
    return jnp.stack(windows_out)
```

```python
import functools

import jax
import jax.numpy as jnp
from jax import lax
from jax.experimental import pallas as pl
from jax.experimental.pallas import tpu as pltpu
from jax.sharding import PartitionSpec as P

LANES = 128
TILE = 16
MESH = pl.DeviceIdType.MESH


def toeplitz_into(target, slot, chunk_rows, chunks, lower):
    for part in range(2):
        previous = jnp.zeros((LANES, LANES), jnp.float32)
        for number in range(chunks + 1):
            if number < chunks:
                row = part * chunks + number
                spread = jnp.broadcast_to(chunk_rows[row : row + 1], (LANES, LANES))
                current = pltpu.roll(spread, 0, 1, stride=1, stride_axis=0)
            else:
                current = jnp.zeros((LANES, LANES), jnp.float32)
            block = jnp.where(lower, current, previous)
            target[slot, pl.ds(number * LANES, LANES), pl.ds(part * LANES, LANES)] = block.astype(
                jnp.bfloat16
            )
            previous = current


def kernel(
    plan,
    owners_ref,
    counts_ref,
    partners_ref,
    stored_ref,
    taps_ref,
    out_ref,
    candidates,
    chosen,
    gathered,
    widened,
    send_taps,
    recv_taps,
    flipped,
    own_toeplitz,
    partner_toeplitz,
    whole_rows,
    half_rows,
    planes,
    totals,
    piece_send,
    piece_recv,
    chosen_send,
    chosen_recv,
    taps_send,
    taps_recv,
):
    width, trials, per, chunks, windows, whole_blocks, half_blocks, piece_rows, hubs = plan
    devices = width * trials
    trial = lax.axis_index("trial")
    column = lax.axis_index("tmpl")
    me = column * trials + trial
    channel_rows = whole_blocks + half_blocks + 2 * chunks
    window_rows = 2 * channel_rows

    def place(flat):
        return (lax.rem(flat, trials), flat // trials)

    def hub_device(hub):
        return hub * devices // hubs

    my_hub = (me * hubs + devices - 1) // devices
    is_hub = hub_device(my_hub) == me
    my_rows = pl.ds(pl.multiple_of(my_hub * piece_rows, TILE), piece_rows)

    barrier = pltpu.get_barrier_semaphore()

    @pl.loop(1, devices)
    def _(step):
        pl.semaphore_signal(
            barrier, inc=1, device_id=place(lax.rem(me + step, devices)), device_id_type=MESH
        )

    pl.semaphore_wait(barrier, devices - 1)

    def piece_copy(hub):
        return pltpu.make_async_remote_copy(
            src_ref=stored_ref.at[pl.ds(pl.multiple_of(hub * piece_rows, TILE), piece_rows)],
            dst_ref=candidates.at[me],
            send_sem=piece_send.at[hub],
            recv_sem=piece_recv.at[me],
            device_id=place(hub_device(hub)),
            device_id_type=MESH,
        )

    @pl.loop(0, hubs)
    def _(step):
        hub = lax.rem(my_hub + step, hubs)

        @pl.when(hub_device(hub) != me)
        def _():
            piece_copy(hub).start()

    @pl.when(is_hub)
    def _():
        candidates[me] = stored_ref[my_rows, :]

    row_number = lax.broadcasted_iota(jnp.int32, (LANES, LANES), 0)
    lane_number = lax.broadcasted_iota(jnp.int32, (LANES, LANES), 1)
    lower = row_number >= lane_number
    flip = ((row_number + lane_number) % LANES == 0).astype(jnp.bfloat16)
    flipped[...] = jnp.dot(taps_ref[...], flip, preferred_element_type=jnp.float32).reshape(
        per, 2 * chunks, LANES
    )

    first = column * per

    @pl.loop(0, width)
    def _(receiver):
        slot = jnp.int32(0)
        for position in range(per):
            named = partners_ref[receiver * per + position] - first
            slot = jnp.where((named >= 0) & (named < per), named, slot)
        rows = flipped[slot]
        send_taps[receiver] = jnp.concatenate([rows, rows], axis=0).astype(jnp.bfloat16)

    def taps_copy(receiver):
        return pltpu.make_async_remote_copy(
            src_ref=send_taps.at[receiver],
            dst_ref=recv_taps.at[column],
            send_sem=taps_send.at[receiver],
            recv_sem=taps_recv.at[column],
            device_id=(trial, receiver),
            device_id_type=MESH,
        )

    @pl.loop(1, width)
    def _(step):
        taps_copy(lax.rem(column + step, width)).start()

    recv_taps[column] = send_taps[column]

    @pl.loop(0, per)
    def _(slot):
        toeplitz_into(own_toeplitz, slot, flipped[slot], chunks, lower)

    def chosen_copy(target):
        return pltpu.make_async_remote_copy(
            src_ref=chosen.at[lax.rem(target, trials)],
            dst_ref=gathered.at[my_rows],
            send_sem=chosen_send.at[target],
            recv_sem=chosen_recv.at[my_hub],
            device_id=place(target),
            device_id_type=MESH,
        )

    @pl.when(is_hub)
    def _():
        @pl.loop(1, devices)
        def _(step):
            other = lax.rem(me + step, devices)
            pltpu.make_async_remote_copy(
                src_ref=candidates.at[other],
                dst_ref=candidates.at[other],
                send_sem=piece_send.at[0],
                recv_sem=piece_recv.at[other],
                device_id=place(other),
                device_id_type=MESH,
            ).wait_recv()

        for which in range(trials):
            for part in range(piece_rows // TILE):
                window = (my_hub * piece_rows + part * TILE) // window_rows
                owner = owners_ref[window, which]
                source = lax.rem(owner, width) * trials + owner // width
                piece = candidates[source]
                chosen[which, pl.ds(part * TILE, TILE), :] = piece[
                    part * TILE : (part + 1) * TILE
                ]

        @pl.loop(1, devices)
        def _(step):
            chosen_copy(lax.rem(me + step, devices)).start()

        gathered[my_rows, :] = chosen[trial]

    @pl.loop(1, width)
    def _(step):
        other = lax.rem(column + step, width)
        pltpu.make_async_remote_copy(
            src_ref=recv_taps.at[other],
            dst_ref=recv_taps.at[other],
            send_sem=taps_send.at[0],
            recv_sem=taps_recv.at[other],
            device_id=(trial, other),
            device_id_type=MESH,
        ).wait_recv()

    @pl.loop(0, per)
    def _(slot):
        source = jnp.maximum(partners_ref[first + slot], 0) // per
        rows = recv_taps[source].astype(jnp.float32)
        toeplitz_into(partner_toeplitz, slot, rows, chunks, lower)

    @pl.loop(0, hubs)
    def _(hub):
        @pl.when(hub_device(hub) != me)
        def _():
            piece = gathered.at[pl.ds(pl.multiple_of(hub * piece_rows, TILE), piece_rows)]
            pltpu.make_async_remote_copy(
                src_ref=piece,
                dst_ref=piece,
                send_sem=chosen_send.at[0],
                recv_sem=chosen_recv.at[hub],
                device_id=place(hub_device(hub)),
                device_id_type=MESH,
            ).wait_recv()

    widened[...] = gathered[...].astype(jnp.float32)
    for pair in range(2 * windows):
        for number in range(chunks + 1):
            lanes = pl.ds(number * LANES, LANES)
            begin = pair * channel_rows + number
            whole_rows[pl.ds(pair * whole_blocks, whole_blocks), lanes] = widened[
                pl.ds(begin, whole_blocks), :
            ].astype(jnp.bfloat16)
            begin += whole_blocks + chunks
            half_rows[pl.ds(pair * half_blocks, half_blocks), lanes] = widened[
                pl.ds(begin, half_blocks), :
            ].astype(jnp.bfloat16)

    def powers_of(rows_ref, matrix, blocks):
        product = jnp.dot(rows_ref[...], matrix, preferred_element_type=jnp.float32)
        result = []
        for window in range(windows):
            real = product[2 * window * blocks : (2 * window + 1) * blocks]
            imag = product[(2 * window + 1) * blocks : (2 * window + 2) * blocks]
            re = real[:, :LANES] - imag[:, LANES:]
            im = real[:, LANES:] + imag[:, :LANES]
            result.append(re * re + im * im)
        return result

    plane_rows = windows * half_blocks

    @pl.loop(0, per)
    def _(slot):
        values = powers_of(half_rows, partner_toeplitz[slot], half_blocks)
        planes[slot] = jnp.concatenate(values, axis=0).astype(jnp.bfloat16)

    doubling_row = lax.broadcasted_iota(jnp.int32, (LANES, 2 * LANES), 0)
    doubling_lane = lax.broadcasted_iota(jnp.int32, (LANES, 2 * LANES), 1)
    doubling = (doubling_row == doubling_lane // 2).astype(jnp.bfloat16)

    @pl.loop(0, per)
    def _(slot):
        doubled = jnp.dot(planes[slot], doubling, preferred_element_type=jnp.float32)
        for window in range(windows):
            base = (window * per + slot) * whole_blocks
            part = doubled[window * half_blocks : (window + 1) * half_blocks]
            for side in range(2):
                totals[pl.ds(base + side, half_blocks, stride=2), :] = part[
                    :, side * LANES : (side + 1) * LANES
                ]

    live = jnp.full((whole_blocks, LANES), counts_ref[column], jnp.int32)

    @pl.loop(0, per)
    def _(slot):
        values = powers_of(whole_rows, own_toeplitz[slot], whole_blocks)
        for window in range(windows):
            base = pl.multiple_of((window * per + slot) * whole_blocks, 8)
            rows = pl.ds(base, whole_blocks)
            totals[rows, :] = jnp.where(live > slot, values[window] + totals[rows, :], 0.0)

    for window in range(windows):
        for block in range(whole_blocks):
            rows = pl.ds(window * per * whole_blocks + block, per, stride=whole_blocks)
            out_ref[window, :, pl.ds(block * LANES, LANES)] = totals[rows, :].astype(jnp.bfloat16)

    @pl.loop(0, hubs)
    def _(hub):
        @pl.when(hub_device(hub) != me)
        def _():
            piece_copy(hub).wait_send()

    @pl.loop(1, width)
    def _(step):
        taps_copy(lax.rem(column + step, width)).wait_send()

    @pl.when(is_hub)
    def _():
        @pl.loop(1, devices)
        def _(step):
            chosen_copy(lax.rem(me + step, devices)).wait_send()


def body(spectra, half_spectra, kernels, owners, counts, partners):
    width = lax.axis_size("tmpl")
    trials = lax.axis_size("trial")
    devices = width * trials
    per, _, taps = kernels.shape
    windows = spectra.shape[0]
    chunks = taps // LANES
    whole_bins = spectra.shape[4] - taps
    whole_blocks = whole_bins // LANES
    half_blocks = (half_spectra.shape[4] - taps) // LANES
    stored = jnp.concatenate([spectra[:, 0, 0], half_spectra[:, 0, 0]], axis=2)
    stored = stored.reshape(-1, LANES)
    tap_rows = kernels.reshape(-1, LANES)
    rows = stored.shape[0]
    tiles = rows // TILE
    piece_tiles = -(-tiles // devices)
    hubs = tiles // piece_tiles
    piece_rows = piece_tiles * TILE
    plan = (width, trials, per, chunks, windows, whole_blocks, half_blocks, piece_rows, hubs)
    span = (chunks + 1) * LANES
    bf16, f32 = jnp.bfloat16, jnp.float32
    dma = pltpu.SemaphoreType.DMA
    smem = pl.BlockSpec(memory_space=pltpu.SMEM)
    vmem = pl.BlockSpec(memory_space=pltpu.VMEM)
    flops = 4 * per * 2 * span * windows * LANES * (whole_blocks + half_blocks)
    powers = pl.pallas_call(
        functools.partial(kernel, plan),
        out_shape=jax.ShapeDtypeStruct((windows, per, whole_bins), bf16),
        in_specs=[smem, smem, smem, vmem, vmem],
        out_specs=vmem,
        scratch_shapes=[
            pltpu.VMEM((devices, piece_rows, LANES), bf16),
            pltpu.VMEM((trials, piece_rows, LANES), bf16),
            pltpu.VMEM((rows, LANES), bf16),
            pltpu.VMEM((rows, LANES), f32),
            pltpu.VMEM((width, 2 * TILE if 2 * chunks > TILE else TILE, LANES), bf16),
            pltpu.VMEM((width, 2 * TILE if 2 * chunks > TILE else TILE, LANES), bf16),
            pltpu.VMEM((per, 2 * chunks, LANES), f32),
            pltpu.VMEM((per, span, 2 * LANES), bf16),
            pltpu.VMEM((per, span, 2 * LANES), bf16),
            pltpu.VMEM((2 * windows * whole_blocks, span), bf16),
            pltpu.VMEM((2 * windows * half_blocks, span), bf16),
            pltpu.VMEM((per, windows * half_blocks, LANES), bf16),
            pltpu.VMEM((windows * per * whole_blocks, LANES), f32),
            dma((hubs,)),
            dma((devices,)),
            dma((devices,)),
            dma((hubs,)),
            dma((width,)),
            dma((width,)),
        ],
        compiler_params=pltpu.CompilerParams(
            collective_id=0, has_side_effects=True, vmem_limit_bytes=48 * 1024 * 1024
        ),
        cost_estimate=pl.CostEstimate(flops=flops, bytes_accessed=2 * powers_size(windows, per, whole_bins), transcendentals=0),
    )(owners, counts, partners, stored, tap_rows)
    return powers[:, None]


def powers_size(windows, per, bins):
    return windows * per * bins


def solution(mesh):
    return jax.shard_map(
        body,
        mesh=mesh,
        in_specs=(
            P(None, "trial", "tmpl", None, None),
            P(None, "trial", "tmpl", None, None),
            P("tmpl", None, None),
            P(),
            P(),
            P(),
        ),
        out_specs=P(None, "trial", "tmpl", None),
        check_vma=False,
    )
```

```python
import functools

import jax
import jax.numpy as jnp
from jax import lax
from jax.experimental import pallas as pl
from jax.experimental.pallas import tpu as pltpu
from jax.sharding import PartitionSpec as P

LANES = 128
TILE = 16
MESH = pl.DeviceIdType.MESH


def toeplitz_into(target, slot, chunk_rows, chunks, lower):
    for part in range(2):
        previous = jnp.zeros((LANES, LANES), jnp.float32)
        for number in range(chunks + 1):
            if number < chunks:
                row = 2 * number + part
                spread = jnp.broadcast_to(chunk_rows[row : row + 1], (LANES, LANES))
                current = pltpu.roll(spread, 0, 1, stride=1, stride_axis=0)
            else:
                current = jnp.zeros((LANES, LANES), jnp.float32)
            block = jnp.where(lower, current, previous)
            target[slot, pl.ds(number * LANES, LANES), pl.ds(part * LANES, LANES)] = block.astype(
                jnp.bfloat16
            )
            previous = current


def kernel(
    plan,
    owners_ref,
    counts_ref,
    partners_ref,
    spectra_ref,
    half_ref,
    taps_ref,
    out_ref,
    stored_ref,
    candidates,
    chosen,
    gathered,
    widened,
    send_taps,
    recv_taps,
    flipped,
    own_toeplitz,
    partner_toeplitz,
    whole_rows,
    half_rows,
    planes,
    doubles,
    totals,
    piece_send,
    piece_recv,
    chosen_send,
    chosen_recv,
    taps_send,
    taps_recv,
):
    width, trials, per, chunks, windows, whole_blocks, half_blocks, piece_rows, hubs = plan
    devices = width * trials
    trial = lax.axis_index("trial")
    column = lax.axis_index("tmpl")
    me = column * trials + trial
    channel_rows = whole_blocks + half_blocks + 2 * chunks
    window_rows = 2 * channel_rows

    def place(flat):
        return (lax.rem(flat, trials), flat // trials)

    def hub_device(hub):
        return hub * devices // hubs

    my_hub = (me * hubs + devices - 1) // devices
    is_hub = hub_device(my_hub) == me
    my_rows = pl.ds(pl.multiple_of(my_hub * piece_rows, TILE), piece_rows)

    barrier = pltpu.get_barrier_semaphore()

    @pl.loop(1, devices)
    def _(step):
        pl.semaphore_signal(
            barrier, inc=1, device_id=place(lax.rem(me + step, devices)), device_id_type=MESH
        )

    for window in range(windows):
        for number in range(channel_rows):
            held, lane = spectra_ref, number * LANES
            if number >= whole_blocks + chunks:
                held, lane = half_ref, (number - whole_blocks - chunks) * LANES
            rows = pl.ds(window * window_rows + number, 2, stride=channel_rows)
            widened[rows, :] = held[window, :, pl.ds(lane, LANES)].astype(jnp.float32)
    stored_ref[...] = widened[...].astype(jnp.bfloat16)

    pl.semaphore_wait(barrier, devices - 1)

    def piece_copy(hub):
        return pltpu.make_async_remote_copy(
            src_ref=stored_ref.at[pl.ds(pl.multiple_of(hub * piece_rows, TILE), piece_rows)],
            dst_ref=candidates.at[me],
            send_sem=piece_send.at[hub],
            recv_sem=piece_recv.at[me],
            device_id=place(hub_device(hub)),
            device_id_type=MESH,
        )

    @pl.loop(0, hubs)
    def _(step):
        hub = lax.rem(my_hub + step, hubs)

        @pl.when(hub_device(hub) != me)
        def _():
            piece_copy(hub).start()

    @pl.when(is_hub)
    def _():
        candidates[me] = stored_ref[my_rows, :]

    row_number = lax.broadcasted_iota(jnp.int32, (LANES, LANES), 0)
    lane_number = lax.broadcasted_iota(jnp.int32, (LANES, LANES), 1)
    lower = row_number >= lane_number
    flip = ((row_number + lane_number) % LANES == 0).astype(jnp.bfloat16)
    for number in range(chunks):
        held = taps_ref[:, :, pl.ds(number * LANES, LANES)].astype(jnp.float32)
        held = held.reshape(2 * per, LANES).astype(jnp.bfloat16)
        turned = jnp.dot(held, flip, preferred_element_type=jnp.float32)
        flipped[:, pl.ds(2 * number, 2), :] = turned.reshape(per, 2, LANES)

    first = column * per

    @pl.loop(0, width)
    def _(receiver):
        slot = jnp.int32(0)
        for position in range(per):
            named = partners_ref[receiver * per + position] - first
            slot = jnp.where((named >= 0) & (named < per), named, slot)
        rows = flipped[slot]
        send_taps[receiver] = jnp.concatenate([rows, rows], axis=0).astype(jnp.bfloat16)

    def taps_copy(receiver):
        return pltpu.make_async_remote_copy(
            src_ref=send_taps.at[receiver],
            dst_ref=recv_taps.at[column],
            send_sem=taps_send.at[receiver],
            recv_sem=taps_recv.at[column],
            device_id=(trial, receiver),
            device_id_type=MESH,
        )

    @pl.loop(1, width)
    def _(step):
        taps_copy(lax.rem(column + step, width)).start()

    recv_taps[column] = send_taps[column]

    @pl.loop(0, per, unroll=2)
    def _(slot):
        toeplitz_into(own_toeplitz, slot, flipped[slot], chunks, lower)

    def chosen_copy(target):
        return pltpu.make_async_remote_copy(
            src_ref=chosen.at[lax.rem(target, trials)],
            dst_ref=gathered.at[my_rows],
            send_sem=chosen_send.at[target],
            recv_sem=chosen_recv.at[my_hub],
            device_id=place(target),
            device_id_type=MESH,
        )

    @pl.when(is_hub)
    def _():
        @pl.loop(1, devices)
        def _(step):
            other = lax.rem(me + step, devices)
            pltpu.make_async_remote_copy(
                src_ref=candidates.at[other],
                dst_ref=candidates.at[other],
                send_sem=piece_send.at[0],
                recv_sem=piece_recv.at[other],
                device_id=place(other),
                device_id_type=MESH,
            ).wait_recv()

        for which in range(trials):
            for part in range(piece_rows // TILE):
                window = (my_hub * piece_rows + part * TILE) // window_rows
                owner = owners_ref[window, which]
                source = lax.rem(owner, width) * trials + owner // width
                piece = candidates[source]
                chosen[which, pl.ds(part * TILE, TILE), :] = piece[
                    part * TILE : (part + 1) * TILE
                ]

        @pl.loop(1, devices)
        def _(step):
            chosen_copy(lax.rem(me + step, devices)).start()

        gathered[my_rows, :] = chosen[trial]

    @pl.loop(1, width)
    def _(step):
        other = lax.rem(column + step, width)
        pltpu.make_async_remote_copy(
            src_ref=recv_taps.at[other],
            dst_ref=recv_taps.at[other],
            send_sem=taps_send.at[0],
            recv_sem=taps_recv.at[other],
            device_id=(trial, other),
            device_id_type=MESH,
        ).wait_recv()

    @pl.loop(0, per, unroll=2)
    def _(slot):
        source = jnp.maximum(partners_ref[first + slot], 0) // per
        rows = recv_taps[source].astype(jnp.float32)
        toeplitz_into(partner_toeplitz, slot, rows, chunks, lower)

    @pl.loop(0, hubs)
    def _(hub):
        @pl.when(hub_device(hub) != me)
        def _():
            piece = gathered.at[pl.ds(pl.multiple_of(hub * piece_rows, TILE), piece_rows)]
            pltpu.make_async_remote_copy(
                src_ref=piece,
                dst_ref=piece,
                send_sem=chosen_send.at[0],
                recv_sem=chosen_recv.at[hub],
                device_id=place(hub_device(hub)),
                device_id_type=MESH,
            ).wait_recv()

    widened[...] = gathered[...].astype(jnp.float32)
    for pair in range(2 * windows):
        for number in range(chunks + 1):
            lanes = pl.ds(number * LANES, LANES)
            begin = pair * channel_rows + number
            whole_rows[pl.ds(pair * whole_blocks, whole_blocks), lanes] = widened[
                pl.ds(begin, whole_blocks), :
            ].astype(jnp.bfloat16)
            begin += whole_blocks + chunks
            half_rows[pl.ds(pair * half_blocks, half_blocks), lanes] = widened[
                pl.ds(begin, half_blocks), :
            ].astype(jnp.bfloat16)

    def powers_of(rows_ref, matrix, blocks):
        product = jnp.dot(rows_ref[...], matrix, preferred_element_type=jnp.float32)
        result = []
        for window in range(windows):
            real = product[2 * window * blocks : (2 * window + 1) * blocks]
            imag = product[(2 * window + 1) * blocks : (2 * window + 2) * blocks]
            re = real[:, :LANES] - imag[:, LANES:]
            im = real[:, LANES:] + imag[:, :LANES]
            result.append(re * re + im * im)
        return result

    plane_rows = windows * half_blocks

    @pl.loop(0, per, unroll=4)
    def _(slot):
        values = powers_of(half_rows, partner_toeplitz[slot], half_blocks)
        planes[slot] = jnp.concatenate(values, axis=0).astype(jnp.bfloat16)

    doubling_row = lax.broadcasted_iota(jnp.int32, (LANES, 2 * LANES), 0)
    doubling_lane = lax.broadcasted_iota(jnp.int32, (LANES, 2 * LANES), 1)
    doubling = (doubling_row == doubling_lane // 2).astype(jnp.bfloat16)

    @pl.loop(0, per, unroll=4)
    def _(slot):
        doubled = jnp.dot(planes[slot], doubling, preferred_element_type=jnp.float32)
        for window in range(windows):
            base = (window * per + slot) * whole_blocks
            part = doubled[window * half_blocks : (window + 1) * half_blocks]
            for side in range(2):
                doubles[pl.ds(base + side, half_blocks, stride=2), :] = part[
                    :, side * LANES : (side + 1) * LANES
                ]

    pitch = per + 1
    live = jnp.full((whole_blocks, LANES), counts_ref[column], jnp.int32)

    @pl.loop(0, per, unroll=2)
    def _(slot):
        values = powers_of(whole_rows, own_toeplitz[slot], whole_blocks)
        for window in range(windows):
            base = pl.multiple_of((window * per + slot) * whole_blocks, 8)
            total = values[window] + doubles[pl.ds(base, whole_blocks), :]
            rows = pl.ds(window * whole_blocks * pitch + slot, whole_blocks, stride=pitch)
            totals[rows, :] = jnp.where(live > slot, total, 0.0)

    for window in range(windows):
        for block in range(whole_blocks):
            rows = pl.ds((window * whole_blocks + block) * pitch, per)
            out_ref[window, :, pl.ds(block * LANES, LANES)] = totals[rows, :].astype(jnp.bfloat16)

    @pl.loop(0, hubs)
    def _(hub):
        @pl.when(hub_device(hub) != me)
        def _():
            piece_copy(hub).wait_send()

    @pl.loop(1, width)
    def _(step):
        taps_copy(lax.rem(column + step, width)).wait_send()

    @pl.when(is_hub)
    def _():
        @pl.loop(1, devices)
        def _(step):
            chosen_copy(lax.rem(me + step, devices)).wait_send()


def body(spectra, half_spectra, kernels, owners, counts, partners):
    width = lax.axis_size("tmpl")
    trials = lax.axis_size("trial")
    devices = width * trials
    per, _, taps = kernels.shape
    windows = spectra.shape[0]
    chunks = taps // LANES
    whole_bins = spectra.shape[4] - taps
    whole_blocks = whole_bins // LANES
    half_blocks = (half_spectra.shape[4] - taps) // LANES
    rows = windows * 2 * (whole_blocks + half_blocks + 2 * chunks)
    tiles = rows // TILE
    piece_tiles = -(-tiles // devices)
    hubs = tiles // piece_tiles
    piece_rows = piece_tiles * TILE
    plan = (width, trials, per, chunks, windows, whole_blocks, half_blocks, piece_rows, hubs)
    span = (chunks + 1) * LANES
    bf16, f32 = jnp.bfloat16, jnp.float32
    dma = pltpu.SemaphoreType.DMA
    smem = pl.BlockSpec(memory_space=pltpu.SMEM)
    vmem = pl.BlockSpec(memory_space=pltpu.VMEM)
    flops = 4 * per * 2 * span * windows * LANES * (whole_blocks + half_blocks)
    powers = pl.pallas_call(
        functools.partial(kernel, plan),
        out_shape=jax.ShapeDtypeStruct((windows, per, whole_bins), bf16),
        in_specs=[smem, smem, smem, vmem, vmem, vmem],
        out_specs=vmem,
        scratch_shapes=[
            pltpu.VMEM((rows, LANES), bf16),
            pltpu.VMEM((devices, piece_rows, LANES), bf16),
            pltpu.VMEM((trials, piece_rows, LANES), bf16),
            pltpu.VMEM((rows, LANES), bf16),
            pltpu.VMEM((rows, LANES), f32),
            pltpu.VMEM((width, 2 * TILE if 2 * chunks > TILE else TILE, LANES), bf16),
            pltpu.VMEM((width, 2 * TILE if 2 * chunks > TILE else TILE, LANES), bf16),
            pltpu.VMEM((per, 2 * chunks, LANES), f32),
            pltpu.VMEM((per, span, 2 * LANES), bf16),
            pltpu.VMEM((per, span, 2 * LANES), bf16),
            pltpu.VMEM((2 * windows * whole_blocks, span), bf16),
            pltpu.VMEM((2 * windows * half_blocks, span), bf16),
            pltpu.VMEM((per, windows * half_blocks, LANES), bf16),
            pltpu.VMEM((windows * per * whole_blocks, LANES), f32),
            pltpu.VMEM((windows * whole_blocks * (per + 1), LANES), f32),
            dma((hubs,)),
            dma((devices,)),
            dma((devices,)),
            dma((hubs,)),
            dma((width,)),
            dma((width,)),
        ],
        compiler_params=pltpu.CompilerParams(
            collective_id=0, has_side_effects=True, vmem_limit_bytes=48 * 1024 * 1024
        ),
        cost_estimate=pl.CostEstimate(flops=flops, bytes_accessed=2 * powers_size(windows, per, whole_bins), transcendentals=0),
    )(owners, counts, partners, spectra[:, 0, 0], half_spectra[:, 0, 0], kernels)
    return powers[:, None]


def powers_size(windows, per, bins):
    return windows * per * bins


def solution(mesh):
    return jax.shard_map(
        body,
        mesh=mesh,
        in_specs=(
            P(None, "trial", "tmpl", None, None),
            P(None, "trial", "tmpl", None, None),
            P("tmpl", None, None),
            P(),
            P(),
            P(),
        ),
        out_specs=P(None, "trial", "tmpl", None),
        check_vma=False,
    )
```

```python
import functools

import jax
import jax.numpy as jnp
from jax import lax
from jax.experimental import pallas as pl
from jax.experimental.pallas import tpu as pltpu
from jax.sharding import PartitionSpec as P

LANES = 128
TILE = 16
MESH = pl.DeviceIdType.MESH


def toeplitz_into(target, slot, chunk_rows, chunks, lower):
    for part in range(2):
        previous = jnp.zeros((LANES, LANES), jnp.float32)
        for number in range(chunks + 1):
            if number < chunks:
                row = 2 * number + part
                spread = jnp.broadcast_to(chunk_rows[row : row + 1], (LANES, LANES))
                current = pltpu.roll(spread, 0, 1, stride=1, stride_axis=0)
            else:
                current = jnp.zeros((LANES, LANES), jnp.float32)
            block = jnp.where(lower, current, previous)
            target[slot, pl.ds(number * LANES, LANES), pl.ds(part * LANES, LANES)] = block.astype(
                jnp.bfloat16
            )
            previous = current


class Stream:
    def __init__(self, devices, windows, blocks, chunks, shift):
        self.devices, self.windows, self.blocks, self.shift = devices, windows, blocks, shift
        self.channel_rows = blocks + chunks
        self.window_rows = 2 * self.channel_rows
        self.rows = windows * self.window_rows
        tiles = -(-self.rows // TILE)
        piece_tiles = -(-tiles // devices)
        self.hubs = -(-tiles // piece_tiles)
        self.piece_rows = piece_tiles * TILE
        self.padded = self.hubs * self.piece_rows

    def scratch(self, trials, span):
        bf16, f32, dma = jnp.bfloat16, jnp.float32, pltpu.SemaphoreType.DMA
        return [
            pltpu.VMEM((self.padded, LANES), bf16),
            pltpu.VMEM((self.devices, self.piece_rows, LANES), bf16),
            pltpu.VMEM((trials, self.piece_rows, LANES), bf16),
            pltpu.VMEM((self.padded, LANES), bf16),
            pltpu.VMEM((self.padded, LANES), f32),
            pltpu.VMEM((2 * self.windows * self.blocks, span), bf16),
            dma((self.hubs,)),
            dma((self.devices,)),
            dma((self.devices,)),
            dma((self.hubs,)),
        ]

    def bind(self, refs, trials, width, trial, me):
        (
            self.stored,
            self.candidates,
            self.chosen,
            self.gathered,
            self.widened,
            self.blocked,
            self.piece_send,
            self.piece_recv,
            self.chosen_send,
            self.chosen_recv,
        ) = refs
        self.trials, self.width, self.trial, self.me = trials, width, trial, me
        turned = lax.rem(me + self.shift, self.devices)
        self.my_hub = (turned * self.hubs + self.devices - 1) // self.devices
        self.is_hub = self.hub_device(self.my_hub) == me
        self.my_rows = self.piece(self.my_hub)

    def hub_device(self, hub):
        place = hub * self.devices // self.hubs
        return lax.rem(place + self.devices - self.shift, self.devices)

    def piece(self, hub):
        return pl.ds(pl.multiple_of(hub * self.piece_rows, TILE), self.piece_rows)

    def place(self, flat):
        return (lax.rem(flat, self.trials), flat // self.trials)

    def lay_out(self, held):
        for window in range(self.windows):
            for number in range(self.channel_rows):
                rows = pl.ds(window * self.window_rows + number, 2, stride=self.channel_rows)
                lanes = pl.ds(number * LANES, LANES)
                self.widened[rows, :] = held[window, :, lanes].astype(jnp.float32)
        rest = self.padded - self.rows
        if rest:
            self.widened[pl.ds(self.rows, rest), :] = jnp.zeros((rest, LANES), jnp.float32)
        self.stored[...] = self.widened[...].astype(jnp.bfloat16)

    def piece_copy(self, hub):
        return pltpu.make_async_remote_copy(
            src_ref=self.stored.at[self.piece(hub)],
            dst_ref=self.candidates.at[self.me],
            send_sem=self.piece_send.at[hub],
            recv_sem=self.piece_recv.at[self.me],
            device_id=self.place(self.hub_device(hub)),
            device_id_type=MESH,
        )

    def each_other_hub(self, act):
        @pl.loop(0, self.hubs)
        def _(step):
            hub = lax.rem(self.my_hub + step, self.hubs)

            @pl.when(self.hub_device(hub) != self.me)
            def _():
                act(hub)

    def each_other_device(self, act):
        @pl.loop(1, self.devices)
        def _(step):
            act(lax.rem(self.me + step, self.devices))

    def scatter(self):
        self.each_other_hub(lambda hub: self.piece_copy(hub).start())

        @pl.when(self.is_hub)
        def _():
            self.candidates[self.me] = self.stored[self.my_rows, :]

    def chosen_copy(self, target):
        return pltpu.make_async_remote_copy(
            src_ref=self.chosen.at[lax.rem(target, self.trials)],
            dst_ref=self.gathered.at[self.my_rows],
            send_sem=self.chosen_send.at[target],
            recv_sem=self.chosen_recv.at[self.my_hub],
            device_id=self.place(target),
            device_id_type=MESH,
        )

    def arrival(self, ref, send_sem, recv_sem, device):
        return pltpu.make_async_remote_copy(
            src_ref=ref,
            dst_ref=ref,
            send_sem=send_sem,
            recv_sem=recv_sem,
            device_id=self.place(device),
            device_id_type=MESH,
        )

    def choose(self, owners_ref):
        @pl.when(self.is_hub)
        def _():
            self.each_other_device(
                lambda other: self.arrival(
                    self.candidates.at[other],
                    self.piece_send.at[0],
                    self.piece_recv.at[other],
                    other,
                ).wait_recv()
            )
            number = lax.broadcasted_iota(jnp.int32, (self.piece_rows, LANES), 0)
            number = number + self.my_hub * self.piece_rows
            for which in range(self.trials):
                kept = None
                for window in range(self.windows):
                    owner = owners_ref[window, which]
                    source = lax.rem(owner, self.width) * self.trials + owner // self.width
                    held = self.candidates[source].astype(jnp.float32)
                    if window:
                        held = jnp.where(number >= window * self.window_rows, held, kept)
                    kept = held
                self.chosen[which] = kept.astype(jnp.bfloat16)

            self.each_other_device(lambda target: self.chosen_copy(target).start())
            self.gathered[self.my_rows, :] = self.chosen[self.trial]

    def collect(self, chunks):
        self.each_other_hub(
            lambda hub: self.arrival(
                self.gathered.at[self.piece(hub)],
                self.chosen_send.at[0],
                self.chosen_recv.at[hub],
                self.hub_device(hub),
            ).wait_recv()
        )
        self.widened[...] = self.gathered[...].astype(jnp.float32)
        for pair in range(2 * self.windows):
            for number in range(chunks + 1):
                begin = pair * self.channel_rows + number
                rows = pl.ds(pair * self.blocks, self.blocks)
                self.blocked[rows, pl.ds(number * LANES, LANES)] = self.widened[
                    pl.ds(begin, self.blocks), :
                ].astype(jnp.bfloat16)

    def finish(self):
        self.each_other_hub(lambda hub: self.piece_copy(hub).wait_send())

        @pl.when(self.is_hub)
        def _():
            self.each_other_device(lambda target: self.chosen_copy(target).wait_send())


def kernel(plan, *refs):
    width, trials, per, chunks, half, whole = plan
    operands, out_ref, refs = refs[:6], refs[6], refs[7:]
    locals_, refs = refs[:6], refs[6:]
    half_refs, whole_refs, refs = refs[:10], refs[10:20], refs[20:]
    owners_ref, counts_ref, partners_ref, spectra_ref, halved_ref, taps_ref = locals_
    (
        send_taps,
        recv_taps,
        flipped,
        own_toeplitz,
        partner_toeplitz,
        planes,
        doubles,
        totals,
        taps_send,
        taps_recv,
        local_sem,
    ) = refs
    windows, whole_blocks, half_blocks = whole.windows, whole.blocks, half.blocks
    devices = width * trials
    trial = lax.axis_index("trial")
    column = lax.axis_index("tmpl")
    me = column * trials + trial
    half.bind(half_refs, trials, width, trial, me)
    whole.bind(whole_refs, trials, width, trial, me)

    local_copies = [
        pltpu.make_async_copy(operands[number], locals_[number], local_sem.at[number])
        for number in range(6)
    ]
    for copy in local_copies:
        copy.start()

    barrier = pltpu.get_barrier_semaphore()

    @pl.loop(1, devices)
    def _(step):
        other = lax.rem(me + step, devices)
        pl.semaphore_signal(barrier, inc=1, device_id=whole.place(other), device_id_type=MESH)

    for copy in local_copies:
        copy.wait()
    half.lay_out(halved_ref)
    whole.lay_out(spectra_ref)

    row_number = lax.broadcasted_iota(jnp.int32, (LANES, LANES), 0)
    lane_number = lax.broadcasted_iota(jnp.int32, (LANES, LANES), 1)
    lower = row_number >= lane_number
    flip = ((row_number + lane_number) % LANES == 0).astype(jnp.bfloat16)
    for number in range(chunks):
        held = taps_ref[:, :, pl.ds(number * LANES, LANES)].astype(jnp.float32)
        held = held.reshape(2 * per, LANES).astype(jnp.bfloat16)
        turned = jnp.dot(held, flip, preferred_element_type=jnp.float32)
        flipped[:, pl.ds(2 * number, 2), :] = turned.reshape(per, 2, LANES)

    first = column * per

    @pl.loop(0, width)
    def _(receiver):
        slot = jnp.int32(0)
        for position in range(per):
            named = partners_ref[receiver * per + position] - first
            slot = jnp.where((named >= 0) & (named < per), named, slot)
        rows = flipped[slot]
        send_taps[receiver] = jnp.concatenate([rows, rows], axis=0).astype(jnp.bfloat16)

    def taps_copy(receiver):
        return pltpu.make_async_remote_copy(
            src_ref=send_taps.at[receiver],
            dst_ref=recv_taps.at[column],
            send_sem=taps_send.at[receiver],
            recv_sem=taps_recv.at[column],
            device_id=(trial, receiver),
            device_id_type=MESH,
        )

    pl.semaphore_wait(barrier, devices - 1)
    half.scatter()
    whole.scatter()

    @pl.loop(1, width)
    def _(step):
        taps_copy(lax.rem(column + step, width)).start()

    recv_taps[column] = send_taps[column]

    def build_own(begin, end):
        @pl.loop(begin, end, unroll=2)
        def _(slot):
            toeplitz_into(own_toeplitz, slot, flipped[slot], chunks, lower)

    build_own(0, per // 2)
    half.choose(owners_ref)
    build_own(per // 2, per)
    whole.choose(owners_ref)

    @pl.loop(1, width)
    def _(step):
        other = lax.rem(column + step, width)
        pltpu.make_async_remote_copy(
            src_ref=recv_taps.at[other],
            dst_ref=recv_taps.at[other],
            send_sem=taps_send.at[0],
            recv_sem=taps_recv.at[other],
            device_id=(trial, other),
            device_id_type=MESH,
        ).wait_recv()

    @pl.loop(0, per, unroll=2)
    def _(slot):
        source = jnp.maximum(partners_ref[first + slot], 0) // per
        rows = recv_taps[source].astype(jnp.float32)
        toeplitz_into(partner_toeplitz, slot, rows, chunks, lower)

    def powers_of(rows_ref, matrix, blocks):
        product = jnp.dot(rows_ref[...], matrix, preferred_element_type=jnp.float32)
        result = []
        for window in range(windows):
            real = product[2 * window * blocks : (2 * window + 1) * blocks]
            imag = product[(2 * window + 1) * blocks : (2 * window + 2) * blocks]
            re = real[:, :LANES] - imag[:, LANES:]
            im = real[:, LANES:] + imag[:, :LANES]
            result.append(re * re + im * im)
        return result

    half.collect(chunks)

    @pl.loop(0, per, unroll=4)
    def _(slot):
        values = powers_of(half.blocked, partner_toeplitz[slot], half_blocks)
        planes[slot] = jnp.concatenate(values, axis=0).astype(jnp.bfloat16)

    doubling_row = lax.broadcasted_iota(jnp.int32, (LANES, 2 * LANES), 0)
    doubling_lane = lax.broadcasted_iota(jnp.int32, (LANES, 2 * LANES), 1)
    doubling = (doubling_row == doubling_lane // 2).astype(jnp.bfloat16)

    @pl.loop(0, per, unroll=4)
    def _(slot):
        doubled = jnp.dot(planes[slot], doubling, preferred_element_type=jnp.float32)
        for window in range(windows):
            base = (window * per + slot) * whole_blocks
            part = doubled[window * half_blocks : (window + 1) * half_blocks]
            for side in range(2):
                doubles[pl.ds(base + side, half_blocks, stride=2), :] = part[
                    :, side * LANES : (side + 1) * LANES
                ]

    whole.collect(chunks)
    pitch = per + 1
    live = jnp.full((whole_blocks, LANES), counts_ref[column], jnp.int32)

    @pl.loop(0, per, unroll=2)
    def _(slot):
        values = powers_of(whole.blocked, own_toeplitz[slot], whole_blocks)
        for window in range(windows):
            base = pl.multiple_of((window * per + slot) * whole_blocks, 8)
            total = values[window] + doubles[pl.ds(base, whole_blocks), :]
            rows = pl.ds(window * whole_blocks * pitch + slot, whole_blocks, stride=pitch)
            totals[rows, :] = jnp.where(live > slot, total, 0.0)

    for window in range(windows):
        for block in range(whole_blocks):
            rows = pl.ds((window * whole_blocks + block) * pitch, per)
            out_ref[window, :, pl.ds(block * LANES, LANES)] = totals[rows, :].astype(jnp.bfloat16)

    @pl.loop(1, width)
    def _(step):
        taps_copy(lax.rem(column + step, width)).wait_send()

    half.finish()
    whole.finish()


def body(spectra, half_spectra, kernels, owners, counts, partners):
    width = lax.axis_size("tmpl")
    trials = lax.axis_size("trial")
    devices = width * trials
    per, _, taps = kernels.shape
    windows = spectra.shape[0]
    chunks = taps // LANES
    whole_bins = spectra.shape[4] - taps
    whole_blocks = whole_bins // LANES
    half_blocks = (half_spectra.shape[4] - taps) // LANES
    half = Stream(devices, windows, half_blocks, chunks, 0)
    whole = Stream(devices, windows, whole_blocks, chunks, 1)
    plan = (width, trials, per, chunks, half, whole)
    span = (chunks + 1) * LANES
    bf16, f32 = jnp.bfloat16, jnp.float32
    dma = pltpu.SemaphoreType.DMA
    operands = (owners, counts, partners, spectra[:, 0, 0], half_spectra[:, 0, 0], kernels)
    near = (pltpu.SMEM, pltpu.SMEM, pltpu.SMEM, pltpu.VMEM, pltpu.VMEM, pltpu.VMEM)
    hbm = pl.BlockSpec(memory_space=pltpu.HBM)
    tap_rows = -(-2 * chunks // TILE) * TILE * (2 if 2 * chunks % TILE == 0 else 1)
    flops = 4 * per * 2 * span * windows * LANES * (whole_blocks + half_blocks)
    powers = pl.pallas_call(
        functools.partial(kernel, plan),
        out_shape=jax.ShapeDtypeStruct((windows, per, whole_bins), bf16),
        in_specs=[hbm] * 6,
        out_specs=pl.BlockSpec(memory_space=pltpu.VMEM),
        scratch_shapes=[
            *[space(held.shape, held.dtype) for space, held in zip(near, operands)],
            *half.scratch(trials, span),
            *whole.scratch(trials, span),
            pltpu.VMEM((width, tap_rows, LANES), bf16),
            pltpu.VMEM((width, tap_rows, LANES), bf16),
            pltpu.VMEM((per, 2 * chunks, LANES), f32),
            pltpu.VMEM((per, span, 2 * LANES), bf16),
            pltpu.VMEM((per, span, 2 * LANES), bf16),
            pltpu.VMEM((per, windows * half_blocks, LANES), bf16),
            pltpu.VMEM((windows * per * whole_blocks, LANES), f32),
            pltpu.VMEM((windows * whole_blocks * (per + 1), LANES), f32),
            dma((width,)),
            dma((width,)),
            dma((6,)),
        ],
        compiler_params=pltpu.CompilerParams(
            collective_id=0, has_side_effects=True, vmem_limit_bytes=48 * 1024 * 1024
        ),
        cost_estimate=pl.CostEstimate(flops=flops, bytes_accessed=2 * windows * per * whole_bins, transcendentals=0),
    )(*operands)
    return powers[:, None]


def solution(mesh):
    return jax.shard_map(
        body,
        mesh=mesh,
        in_specs=(
            P(None, "trial", "tmpl", None, None),
            P(None, "trial", "tmpl", None, None),
            P("tmpl", None, None),
            P(),
            P(),
            P(),
        ),
        out_specs=P(None, "trial", "tmpl", None),
        check_vma=False,
    )
```

```python
import functools

import jax
import jax.numpy as jnp
from jax import lax
from jax.experimental import pallas as pl
from jax.experimental.pallas import tpu as pltpu
from jax.sharding import PartitionSpec as P

LANES = 128
TILE = 16
MESH = pl.DeviceIdType.MESH


def toeplitz_into(target, slot, chunk_rows, chunks, lower):
    for part in range(2):
        previous = jnp.zeros((LANES, LANES), jnp.float32)
        for number in range(chunks + 1):
            if number < chunks:
                row = 2 * number + part
                spread = jnp.broadcast_to(chunk_rows[row : row + 1], (LANES, LANES))
                current = pltpu.roll(spread, 0, 1, stride=1, stride_axis=0)
            else:
                current = jnp.zeros((LANES, LANES), jnp.float32)
            block = jnp.where(lower, current, previous)
            target[slot, pl.ds(number * LANES, LANES), pl.ds(part * LANES, LANES)] = block.astype(
                jnp.bfloat16
            )
            previous = current


SPREAD = 5


class Stream:
    def __init__(self, group, windows, blocks, chunks, first_hub, most_hubs):
        self.group, self.windows, self.blocks, self.first_hub = group, windows, blocks, first_hub
        self.channel_rows = blocks + chunks
        self.window_rows = 2 * self.channel_rows
        self.rows = windows * self.window_rows
        tiles = -(-self.rows // TILE)
        piece_tiles = -(-tiles // most_hubs)
        self.hubs = -(-tiles // piece_tiles)
        self.piece_rows = piece_tiles * TILE
        self.padded = self.hubs * self.piece_rows

    def scratch(self, trials, span):
        bf16, f32, dma = jnp.bfloat16, jnp.float32, pltpu.SemaphoreType.DMA
        return [
            pltpu.VMEM((self.padded, LANES), bf16),
            pltpu.VMEM((self.group, self.piece_rows, LANES), bf16),
            pltpu.VMEM((trials, self.piece_rows, LANES), bf16),
            pltpu.VMEM((trials, self.piece_rows, LANES), bf16),
            pltpu.VMEM((trials, self.piece_rows, LANES), bf16),
            pltpu.VMEM((self.padded, LANES), bf16),
            pltpu.VMEM((self.padded, LANES), f32),
            pltpu.VMEM((2 * self.windows * self.blocks, span), bf16),
            dma((self.hubs,)),
            dma((self.group,)),
            dma((2,)),
            dma((self.group,)),
            dma((self.hubs,)),
        ]

    def bind(self, refs, trials, width, trial, me):
        (
            self.stored,
            self.candidates,
            self.chosen,
            self.across,
            self.settled,
            self.gathered,
            self.widened,
            self.blocked,
            self.piece_send,
            self.piece_recv,
            self.swap_sem,
            self.chosen_send,
            self.chosen_recv,
        ) = refs
        self.trials, self.width, self.trial, self.me = trials, width, trial, me
        self.my_group = me // self.group
        self.local = lax.rem(me, self.group)
        back = pow(SPREAD, -1, self.group)
        turn = lax.rem(self.local * back + self.group - self.first_hub, self.group)
        self.is_hub = turn < self.hubs
        self.my_hub = jnp.minimum(turn, self.hubs - 1)
        self.my_rows = self.piece(self.my_hub)

    def hub_local(self, hub):
        return lax.rem((hub + self.first_hub) * SPREAD, self.group)

    def piece(self, hub):
        return pl.ds(pl.multiple_of(hub * self.piece_rows, TILE), self.piece_rows)

    def place(self, flat):
        return (lax.rem(flat, self.trials), flat // self.trials)

    def near(self, local):
        return self.place(self.my_group * self.group + local)

    def lay_out(self, held):
        for window in range(self.windows):
            for number in range(self.channel_rows):
                rows = pl.ds(window * self.window_rows + number, 2, stride=self.channel_rows)
                lanes = pl.ds(number * LANES, LANES)
                self.widened[rows, :] = held[window, :, lanes].astype(jnp.float32)
        rest = self.padded - self.rows
        if rest:
            self.widened[pl.ds(self.rows, rest), :] = jnp.zeros((rest, LANES), jnp.float32)
        self.stored[...] = self.widened[...].astype(jnp.bfloat16)

    def piece_copy(self, hub):
        return pltpu.make_async_remote_copy(
            src_ref=self.stored.at[self.piece(hub)],
            dst_ref=self.candidates.at[self.local],
            send_sem=self.piece_send.at[hub],
            recv_sem=self.piece_recv.at[self.local],
            device_id=self.near(self.hub_local(hub)),
            device_id_type=MESH,
        )

    def each_other_hub(self, act):
        @pl.loop(0, self.hubs)
        def _(step):
            hub = lax.rem(self.local + step, self.hubs)

            @pl.when(self.hub_local(hub) != self.local)
            def _():
                act(hub)

    def each_other_device(self, act):
        @pl.loop(1, self.group)
        def _(step):
            act(lax.rem(self.local + step, self.group))

    def scatter(self):
        self.each_other_hub(lambda hub: self.piece_copy(hub).start())

        @pl.when(self.is_hub)
        def _():
            self.candidates[self.local] = self.stored[self.my_rows, :]

    def chosen_copy(self, target):
        return pltpu.make_async_remote_copy(
            src_ref=self.settled.at[lax.rem(target, self.trials)],
            dst_ref=self.gathered.at[self.my_rows],
            send_sem=self.chosen_send.at[target],
            recv_sem=self.chosen_recv.at[self.my_hub],
            device_id=self.near(target),
            device_id_type=MESH,
        )

    def arrival(self, ref, send_sem, recv_sem, device):
        return pltpu.make_async_remote_copy(
            src_ref=ref,
            dst_ref=ref,
            send_sem=send_sem,
            recv_sem=recv_sem,
            device_id=self.near(device),
            device_id_type=MESH,
        )

    def by_window(self, take):
        number = lax.broadcasted_iota(jnp.int32, (self.piece_rows, LANES), 0)
        number = number + self.my_hub * self.piece_rows
        kept = take(0)
        for window in range(1, self.windows):
            kept = jnp.where(number >= window * self.window_rows, take(window), kept)
        return kept.astype(jnp.bfloat16)

    def flat_owner(self, owners_ref, window, which):
        owner = owners_ref[window, which]
        return lax.rem(owner, self.width) * self.trials + owner // self.width

    def swap_copy(self):
        return pltpu.make_async_remote_copy(
            src_ref=self.chosen,
            dst_ref=self.across,
            send_sem=self.swap_sem.at[0],
            recv_sem=self.swap_sem.at[1],
            device_id=self.place(lax.rem(self.me + self.group, 2 * self.group)),
            device_id_type=MESH,
        )

    def choose(self, owners_ref):
        @pl.when(self.is_hub)
        def _():
            self.each_other_device(
                lambda other: self.arrival(
                    self.candidates.at[other],
                    self.piece_send.at[0],
                    self.piece_recv.at[other],
                    other,
                ).wait_recv()
            )
            for which in range(self.trials):

                def take(window):
                    source = lax.rem(self.flat_owner(owners_ref, window, which), self.group)
                    return self.candidates[source].astype(jnp.float32)

                self.chosen[which] = self.by_window(take)
            self.swap_copy().start()

    def settle(self, owners_ref):
        @pl.when(self.is_hub)
        def _():
            self.swap_copy().wait()
            shape = (self.piece_rows, LANES)
            for which in range(self.trials):
                mine = self.chosen[which].astype(jnp.float32)
                theirs = self.across[which].astype(jnp.float32)

                def take(window):
                    holder = self.flat_owner(owners_ref, window, which) // self.group
                    return jnp.where(jnp.full(shape, holder) == self.my_group, mine, theirs)

                self.settled[which] = self.by_window(take)
            self.each_other_device(lambda target: self.chosen_copy(target).start())
            self.gathered[self.my_rows, :] = self.settled[self.trial]

    def collect(self, chunks):
        self.each_other_hub(
            lambda hub: self.arrival(
                self.gathered.at[self.piece(hub)],
                self.chosen_send.at[0],
                self.chosen_recv.at[hub],
                self.hub_local(hub),
            ).wait_recv()
        )
        self.widened[...] = self.gathered[...].astype(jnp.float32)
        for pair in range(2 * self.windows):
            for number in range(chunks + 1):
                begin = pair * self.channel_rows + number
                rows = pl.ds(pair * self.blocks, self.blocks)
                self.blocked[rows, pl.ds(number * LANES, LANES)] = self.widened[
                    pl.ds(begin, self.blocks), :
                ].astype(jnp.bfloat16)

    def finish(self):
        self.each_other_hub(lambda hub: self.piece_copy(hub).wait_send())

        @pl.when(self.is_hub)
        def _():
            self.each_other_device(lambda target: self.chosen_copy(target).wait_send())


def kernel(plan, *refs):
    width, trials, per, chunks, half, whole = plan
    operands, out_ref, refs = refs[:6], refs[6], refs[7:]
    locals_, refs = refs[:6], refs[6:]
    half_refs, whole_refs, refs = refs[:13], refs[13:26], refs[26:]
    owners_ref, counts_ref, partners_ref, spectra_ref, halved_ref, taps_ref = locals_
    (
        send_taps,
        recv_taps,
        flipped,
        own_toeplitz,
        partner_toeplitz,
        planes,
        doubles,
        totals,
        taps_send,
        taps_recv,
        local_sem,
    ) = refs
    windows, whole_blocks, half_blocks = whole.windows, whole.blocks, half.blocks
    trial = lax.axis_index("trial")
    column = lax.axis_index("tmpl")
    me = column * trials + trial
    half.bind(half_refs, trials, width, trial, me)
    whole.bind(whole_refs, trials, width, trial, me)

    local_copies = [
        pltpu.make_async_copy(operands[number], locals_[number], local_sem.at[number])
        for number in range(6)
    ]
    for copy in local_copies:
        copy.start()

    barrier = pltpu.get_barrier_semaphore()

    def greet(place):
        pl.semaphore_signal(barrier, inc=1, device_id=place, device_id_type=MESH)

    far_column = (1 - me // whole.group) * (width // 2)
    whole.each_other_device(lambda other: greet(whole.near(other)))

    @pl.loop(0, width // 2)
    def _(step):
        greet((trial, far_column + step))

    for copy in local_copies:
        copy.wait()
    half.lay_out(halved_ref)
    whole.lay_out(spectra_ref)

    row_number = lax.broadcasted_iota(jnp.int32, (LANES, LANES), 0)
    lane_number = lax.broadcasted_iota(jnp.int32, (LANES, LANES), 1)
    lower = row_number >= lane_number
    flip = ((row_number + lane_number) % LANES == 0).astype(jnp.bfloat16)
    for number in range(chunks):
        held = taps_ref[:, :, pl.ds(number * LANES, LANES)].astype(jnp.float32)
        held = held.reshape(2 * per, LANES).astype(jnp.bfloat16)
        turned = jnp.dot(held, flip, preferred_element_type=jnp.float32)
        flipped[:, pl.ds(2 * number, 2), :] = turned.reshape(per, 2, LANES)

    first = column * per

    @pl.loop(0, width)
    def _(receiver):
        slot = jnp.int32(0)
        for position in range(per):
            named = partners_ref[receiver * per + position] - first
            slot = jnp.where((named >= 0) & (named < per), named, slot)
        rows = flipped[slot]
        send_taps[receiver] = jnp.concatenate([rows, rows], axis=0).astype(jnp.bfloat16)

    def taps_copy(receiver):
        return pltpu.make_async_remote_copy(
            src_ref=send_taps.at[receiver],
            dst_ref=recv_taps.at[column],
            send_sem=taps_send.at[receiver],
            recv_sem=taps_recv.at[column],
            device_id=(trial, receiver),
            device_id_type=MESH,
        )

    pl.semaphore_wait(barrier, whole.group - 1 + width // 2)
    half.scatter()
    whole.scatter()

    @pl.loop(1, width)
    def _(step):
        taps_copy(lax.rem(column + step, width)).start()

    recv_taps[column] = send_taps[column]

    def build_own(begin, end):
        @pl.loop(begin, end, unroll=2)
        def _(slot):
            toeplitz_into(own_toeplitz, slot, flipped[slot], chunks, lower)

    build_own(0, per // 2)
    half.choose(owners_ref)
    build_own(per // 2, 3 * per // 4)
    half.settle(owners_ref)
    whole.choose(owners_ref)
    build_own(3 * per // 4, per)
    whole.settle(owners_ref)

    @pl.loop(1, width)
    def _(step):
        other = lax.rem(column + step, width)
        pltpu.make_async_remote_copy(
            src_ref=recv_taps.at[other],
            dst_ref=recv_taps.at[other],
            send_sem=taps_send.at[0],
            recv_sem=taps_recv.at[other],
            device_id=(trial, other),
            device_id_type=MESH,
        ).wait_recv()

    @pl.loop(0, per, unroll=2)
    def _(slot):
        source = jnp.maximum(partners_ref[first + slot], 0) // per
        rows = recv_taps[source].astype(jnp.float32)
        toeplitz_into(partner_toeplitz, slot, rows, chunks, lower)

    def powers_of(rows_ref, matrix, blocks):
        product = jnp.dot(rows_ref[...], matrix, preferred_element_type=jnp.float32)
        result = []
        for window in range(windows):
            real = product[2 * window * blocks : (2 * window + 1) * blocks]
            imag = product[(2 * window + 1) * blocks : (2 * window + 2) * blocks]
            re = real[:, :LANES] - imag[:, LANES:]
            im = real[:, LANES:] + imag[:, :LANES]
            result.append(re * re + im * im)
        return result

    half.collect(chunks)

    @pl.loop(0, per, unroll=4)
    def _(slot):
        values = powers_of(half.blocked, partner_toeplitz[slot], half_blocks)
        planes[slot] = jnp.concatenate(values, axis=0).astype(jnp.bfloat16)

    doubling_row = lax.broadcasted_iota(jnp.int32, (LANES, 2 * LANES), 0)
    doubling_lane = lax.broadcasted_iota(jnp.int32, (LANES, 2 * LANES), 1)
    doubling = (doubling_row == doubling_lane // 2).astype(jnp.bfloat16)

    @pl.loop(0, per, unroll=4)
    def _(slot):
        doubled = jnp.dot(planes[slot], doubling, preferred_element_type=jnp.float32)
        for window in range(windows):
            base = (window * per + slot) * whole_blocks
            part = doubled[window * half_blocks : (window + 1) * half_blocks]
            for side in range(2):
                doubles[pl.ds(base + side, half_blocks, stride=2), :] = part[
                    :, side * LANES : (side + 1) * LANES
                ]

    whole.collect(chunks)
    pitch = per + 1
    live = jnp.full((whole_blocks, LANES), counts_ref[column], jnp.int32)

    @pl.loop(0, per, unroll=2)
    def _(slot):
        values = powers_of(whole.blocked, own_toeplitz[slot], whole_blocks)
        for window in range(windows):
            base = pl.multiple_of((window * per + slot) * whole_blocks, 8)
            total = values[window] + doubles[pl.ds(base, whole_blocks), :]
            rows = pl.ds(window * whole_blocks * pitch + slot, whole_blocks, stride=pitch)
            totals[rows, :] = jnp.where(live > slot, total, 0.0)

    for window in range(windows):
        for block in range(whole_blocks):
            rows = pl.ds((window * whole_blocks + block) * pitch, per)
            out_ref[window, :, pl.ds(block * LANES, LANES)] = totals[rows, :].astype(jnp.bfloat16)

    @pl.loop(1, width)
    def _(step):
        taps_copy(lax.rem(column + step, width)).wait_send()

    half.finish()
    whole.finish()


def body(spectra, half_spectra, kernels, owners, counts, partners):
    width = lax.axis_size("tmpl")
    trials = lax.axis_size("trial")
    group = width * trials // 2
    per, _, taps = kernels.shape
    windows = spectra.shape[0]
    chunks = taps // LANES
    whole_bins = spectra.shape[4] - taps
    whole_blocks = whole_bins // LANES
    half_blocks = (half_spectra.shape[4] - taps) // LANES
    half_hubs = max(1, group * (half_blocks + chunks) // (whole_blocks + half_blocks + 2 * chunks))
    half = Stream(group, windows, half_blocks, chunks, 0, half_hubs)
    whole = Stream(group, windows, whole_blocks, chunks, half.hubs, group - half.hubs)
    plan = (width, trials, per, chunks, half, whole)
    span = (chunks + 1) * LANES
    bf16, f32 = jnp.bfloat16, jnp.float32
    dma = pltpu.SemaphoreType.DMA
    operands = (owners, counts, partners, spectra[:, 0, 0], half_spectra[:, 0, 0], kernels)
    near = (pltpu.SMEM, pltpu.SMEM, pltpu.SMEM, pltpu.VMEM, pltpu.VMEM, pltpu.VMEM)
    hbm = pl.BlockSpec(memory_space=pltpu.HBM)
    tap_rows = -(-2 * chunks // TILE) * TILE * (2 if 2 * chunks % TILE == 0 else 1)
    flops = 4 * per * 2 * span * windows * LANES * (whole_blocks + half_blocks)
    powers = pl.pallas_call(
        functools.partial(kernel, plan),
        out_shape=jax.ShapeDtypeStruct((windows, per, whole_bins), bf16),
        in_specs=[hbm] * 6,
        out_specs=pl.BlockSpec(memory_space=pltpu.VMEM),
        scratch_shapes=[
            *[space(held.shape, held.dtype) for space, held in zip(near, operands)],
            *half.scratch(trials, span),
            *whole.scratch(trials, span),
            pltpu.VMEM((width, tap_rows, LANES), bf16),
            pltpu.VMEM((width, tap_rows, LANES), bf16),
            pltpu.VMEM((per, 2 * chunks, LANES), f32),
            pltpu.VMEM((per, span, 2 * LANES), bf16),
            pltpu.VMEM((per, span, 2 * LANES), bf16),
            pltpu.VMEM((per, windows * half_blocks, LANES), bf16),
            pltpu.VMEM((windows * per * whole_blocks, LANES), f32),
            pltpu.VMEM((windows * whole_blocks * (per + 1), LANES), f32),
            dma((width,)),
            dma((width,)),
            dma((6,)),
        ],
        compiler_params=pltpu.CompilerParams(
            collective_id=0, has_side_effects=True, vmem_limit_bytes=56 * 1024 * 1024
        ),
        cost_estimate=pl.CostEstimate(flops=flops, bytes_accessed=2 * windows * per * whole_bins, transcendentals=0),
    )(*operands)
    return powers[:, None]


def solution(mesh):
    return jax.shard_map(
        body,
        mesh=mesh,
        in_specs=(
            P(None, "trial", "tmpl", None, None),
            P(None, "trial", "tmpl", None, None),
            P("tmpl", None, None),
            P(),
            P(),
            P(),
        ),
        out_specs=P(None, "trial", "tmpl", None),
        check_vma=False,
    )
```

```python
import functools

import jax
import jax.numpy as jnp
from jax import lax
from jax.experimental import pallas as pl
from jax.experimental.pallas import tpu as pltpu
from jax.sharding import PartitionSpec as P

LANES = 128
TILE = 16
MESH = pl.DeviceIdType.MESH


def toeplitz_into(target, slot, chunk_rows, chunks, masks):
    zero = jnp.zeros((TILE, LANES), jnp.bfloat16)
    steps = LANES // TILE
    for part in range(2):
        previous = [zero] * steps
        for number in range(chunks + 1):
            current = [zero] * steps
            if number < chunks:
                row = 2 * number + part
                spread = jnp.broadcast_to(chunk_rows[row : row + 1], (TILE, LANES))
                turned = pltpu.roll(spread, 0, 1, stride=1, stride_axis=0).astype(jnp.bfloat16)
                current = [turned] + [
                    pltpu.roll(turned, step * TILE, 1) for step in range(1, steps)
                ]
            for step in range(steps):
                block = jnp.where(masks[step], current[step], previous[step])
                rows = pl.ds(number * LANES + step * TILE, TILE)
                target[slot, rows, pl.ds(part * LANES, LANES)] = block
            previous = current


SPREAD = 5


class Stream:
    def __init__(self, group, windows, blocks, chunks, first_hub, most_hubs):
        self.group, self.windows, self.blocks, self.first_hub = group, windows, blocks, first_hub
        self.channel_rows = blocks + chunks
        self.window_rows = 2 * self.channel_rows
        self.rows = windows * self.window_rows
        tiles = -(-self.rows // TILE)
        piece_tiles = -(-tiles // most_hubs)
        self.hubs = -(-tiles // piece_tiles)
        self.piece_rows = piece_tiles * TILE
        self.padded = self.hubs * self.piece_rows

    def scratch(self, trials, span):
        bf16, f32, dma = jnp.bfloat16, jnp.float32, pltpu.SemaphoreType.DMA
        return [
            pltpu.VMEM((self.padded, LANES), bf16),
            pltpu.VMEM((self.group, self.piece_rows, LANES), bf16),
            pltpu.VMEM((trials, self.piece_rows, LANES), bf16),
            pltpu.VMEM((trials, self.piece_rows, LANES), bf16),
            pltpu.VMEM((trials, self.piece_rows, LANES), bf16),
            pltpu.VMEM((self.padded, LANES), bf16),
            pltpu.VMEM((self.padded, LANES), f32),
            pltpu.VMEM((2 * self.windows * self.blocks, span), bf16),
            dma((self.hubs,)),
            dma((self.group,)),
            dma((2,)),
            dma((self.group,)),
            dma((self.hubs,)),
        ]

    def bind(self, refs, trials, width, trial, me):
        (
            self.stored,
            self.candidates,
            self.chosen,
            self.across,
            self.settled,
            self.gathered,
            self.widened,
            self.blocked,
            self.piece_send,
            self.piece_recv,
            self.swap_sem,
            self.chosen_send,
            self.chosen_recv,
        ) = refs
        self.trials, self.width, self.trial, self.me = trials, width, trial, me
        self.my_group = me // self.group
        self.local = lax.rem(me, self.group)
        back = pow(SPREAD, -1, self.group)
        turn = lax.rem(self.local * back + self.group - self.first_hub, self.group)
        self.is_hub = turn < self.hubs
        self.my_hub = jnp.minimum(turn, self.hubs - 1)
        self.my_rows = self.piece(self.my_hub)

    def hub_local(self, hub):
        return lax.rem((hub + self.first_hub) * SPREAD, self.group)

    def piece(self, hub):
        return pl.ds(pl.multiple_of(hub * self.piece_rows, TILE), self.piece_rows)

    def place(self, flat):
        return (lax.rem(flat, self.trials), flat // self.trials)

    def near(self, local):
        return self.place(self.my_group * self.group + local)

    def lay_out(self, held):
        for window in range(self.windows):
            for number in range(self.channel_rows):
                rows = pl.ds(window * self.window_rows + number, 2, stride=self.channel_rows)
                lanes = pl.ds(number * LANES, LANES)
                self.widened[rows, :] = held[window, :, lanes].astype(jnp.float32)
        rest = self.padded - self.rows
        if rest:
            self.widened[pl.ds(self.rows, rest), :] = jnp.zeros((rest, LANES), jnp.float32)
        self.stored[...] = self.widened[...].astype(jnp.bfloat16)

    def piece_copy(self, hub):
        return pltpu.make_async_remote_copy(
            src_ref=self.stored.at[self.piece(hub)],
            dst_ref=self.candidates.at[self.local],
            send_sem=self.piece_send.at[hub],
            recv_sem=self.piece_recv.at[self.local],
            device_id=self.near(self.hub_local(hub)),
            device_id_type=MESH,
        )

    def each_other_hub(self, act):
        @pl.loop(0, self.hubs)
        def _(step):
            hub = lax.rem(self.local + step, self.hubs)

            @pl.when(self.hub_local(hub) != self.local)
            def _():
                act(hub)

    def each_other_device(self, act):
        @pl.loop(1, self.group)
        def _(step):
            act(lax.rem(self.local + step, self.group))

    def scatter(self):
        self.each_other_hub(lambda hub: self.piece_copy(hub).start())

        @pl.when(self.is_hub)
        def _():
            self.candidates[self.local] = self.stored[self.my_rows, :]

    def chosen_copy(self, target):
        return pltpu.make_async_remote_copy(
            src_ref=self.settled.at[lax.rem(target, self.trials)],
            dst_ref=self.gathered.at[self.my_rows],
            send_sem=self.chosen_send.at[target],
            recv_sem=self.chosen_recv.at[self.my_hub],
            device_id=self.near(target),
            device_id_type=MESH,
        )

    def arrival(self, ref, send_sem, recv_sem, device):
        return pltpu.make_async_remote_copy(
            src_ref=ref,
            dst_ref=ref,
            send_sem=send_sem,
            recv_sem=recv_sem,
            device_id=self.near(device),
            device_id_type=MESH,
        )

    def by_window(self, take):
        number = lax.broadcasted_iota(jnp.int32, (self.piece_rows, LANES), 0)
        number = number + self.my_hub * self.piece_rows
        kept = take(0)
        for window in range(1, self.windows):
            kept = jnp.where(number >= window * self.window_rows, take(window), kept)
        return kept.astype(jnp.bfloat16)

    def flat_owner(self, owners_ref, window, which):
        owner = owners_ref[window, which]
        return lax.rem(owner, self.width) * self.trials + owner // self.width

    def swap_copy(self):
        return pltpu.make_async_remote_copy(
            src_ref=self.chosen,
            dst_ref=self.across,
            send_sem=self.swap_sem.at[0],
            recv_sem=self.swap_sem.at[1],
            device_id=self.place(lax.rem(self.me + self.group, 2 * self.group)),
            device_id_type=MESH,
        )

    def choose(self, owners_ref):
        @pl.when(self.is_hub)
        def _():
            self.each_other_device(
                lambda other: self.arrival(
                    self.candidates.at[other],
                    self.piece_send.at[0],
                    self.piece_recv.at[other],
                    other,
                ).wait_recv()
            )
            for which in range(self.trials):

                def take(window):
                    source = lax.rem(self.flat_owner(owners_ref, window, which), self.group)
                    return self.candidates[source].astype(jnp.float32)

                self.chosen[which] = self.by_window(take)
            self.swap_copy().start()

    def settle(self, owners_ref):
        @pl.when(self.is_hub)
        def _():
            self.swap_copy().wait()
            shape = (self.piece_rows, LANES)
            for which in range(self.trials):
                mine = self.chosen[which].astype(jnp.float32)
                theirs = self.across[which].astype(jnp.float32)

                def take(window):
                    holder = self.flat_owner(owners_ref, window, which) // self.group
                    return jnp.where(jnp.full(shape, holder) == self.my_group, mine, theirs)

                self.settled[which] = self.by_window(take)
            self.each_other_device(lambda target: self.chosen_copy(target).start())
            self.gathered[self.my_rows, :] = self.settled[self.trial]

    def collect(self, chunks):
        self.each_other_hub(
            lambda hub: self.arrival(
                self.gathered.at[self.piece(hub)],
                self.chosen_send.at[0],
                self.chosen_recv.at[hub],
                self.hub_local(hub),
            ).wait_recv()
        )
        self.widened[...] = self.gathered[...].astype(jnp.float32)
        for pair in range(2 * self.windows):
            for number in range(chunks + 1):
                begin = pair * self.channel_rows + number
                rows = pl.ds(pair * self.blocks, self.blocks)
                self.blocked[rows, pl.ds(number * LANES, LANES)] = self.widened[
                    pl.ds(begin, self.blocks), :
                ].astype(jnp.bfloat16)

    def finish(self):
        self.each_other_hub(lambda hub: self.piece_copy(hub).wait_send())

        @pl.when(self.is_hub)
        def _():
            self.each_other_device(lambda target: self.chosen_copy(target).wait_send())


def kernel(plan, *refs):
    width, trials, per, chunks, half, whole = plan
    operands, out_ref, refs = refs[:6], refs[6], refs[7:]
    locals_, refs = refs[:6], refs[6:]
    half_refs, whole_refs, refs = refs[:13], refs[13:26], refs[26:]
    owners_ref, counts_ref, partners_ref, spectra_ref, halved_ref, taps_ref = locals_
    (
        send_taps,
        recv_taps,
        flipped,
        own_toeplitz,
        partner_toeplitz,
        planes,
        doubles,
        totals,
        taps_send,
        taps_recv,
        local_sem,
    ) = refs
    windows, whole_blocks, half_blocks = whole.windows, whole.blocks, half.blocks
    trial = lax.axis_index("trial")
    column = lax.axis_index("tmpl")
    me = column * trials + trial
    half.bind(half_refs, trials, width, trial, me)
    whole.bind(whole_refs, trials, width, trial, me)

    local_copies = [
        pltpu.make_async_copy(operands[number], locals_[number], local_sem.at[number])
        for number in range(6)
    ]
    for copy in local_copies:
        copy.start()

    barrier = pltpu.get_barrier_semaphore()

    def greet(place):
        pl.semaphore_signal(barrier, inc=1, device_id=place, device_id_type=MESH)

    far_column = (1 - me // whole.group) * (width // 2)
    whole.each_other_device(lambda other: greet(whole.near(other)))

    @pl.loop(0, width // 2)
    def _(step):
        greet((trial, far_column + step))

    for copy in local_copies:
        copy.wait()
    half.lay_out(halved_ref)
    whole.lay_out(spectra_ref)

    row_number = lax.broadcasted_iota(jnp.int32, (LANES, LANES), 0)
    lane_number = lax.broadcasted_iota(jnp.int32, (LANES, LANES), 1)
    masks = [
        row_number[step * TILE : (step + 1) * TILE] >= lane_number[:TILE]
        for step in range(LANES // TILE)
    ]
    flip = ((row_number + lane_number) % LANES == 0).astype(jnp.bfloat16)
    for number in range(chunks):
        held = taps_ref[:, :, pl.ds(number * LANES, LANES)].astype(jnp.float32)
        held = held.reshape(2 * per, LANES).astype(jnp.bfloat16)
        turned = jnp.dot(held, flip, preferred_element_type=jnp.float32)
        flipped[:, pl.ds(2 * number, 2), :] = turned.reshape(per, 2, LANES)

    first = column * per

    @pl.loop(0, width)
    def _(receiver):
        slot = jnp.int32(0)
        for position in range(per):
            named = partners_ref[receiver * per + position] - first
            slot = jnp.where((named >= 0) & (named < per), named, slot)
        rows = flipped[slot]
        send_taps[receiver] = jnp.concatenate([rows, rows], axis=0).astype(jnp.bfloat16)

    def taps_copy(receiver):
        return pltpu.make_async_remote_copy(
            src_ref=send_taps.at[receiver],
            dst_ref=recv_taps.at[column],
            send_sem=taps_send.at[receiver],
            recv_sem=taps_recv.at[column],
            device_id=(trial, receiver),
            device_id_type=MESH,
        )

    pl.semaphore_wait(barrier, whole.group - 1 + width // 2)
    half.scatter()
    whole.scatter()

    @pl.loop(1, width)
    def _(step):
        taps_copy(lax.rem(column + step, width)).start()

    recv_taps[column] = send_taps[column]

    def build_own(begin, end):
        @pl.loop(begin, end, unroll=2)
        def _(slot):
            toeplitz_into(own_toeplitz, slot, flipped[slot], chunks, masks)

    build_own(0, per // 2)
    half.choose(owners_ref)
    build_own(per // 2, 3 * per // 4)
    half.settle(owners_ref)
    whole.choose(owners_ref)
    build_own(3 * per // 4, per)
    whole.settle(owners_ref)

    @pl.loop(1, width)
    def _(step):
        other = lax.rem(column + step, width)
        pltpu.make_async_remote_copy(
            src_ref=recv_taps.at[other],
            dst_ref=recv_taps.at[other],
            send_sem=taps_send.at[0],
            recv_sem=taps_recv.at[other],
            device_id=(trial, other),
            device_id_type=MESH,
        ).wait_recv()

    @pl.loop(0, per, unroll=2)
    def _(slot):
        source = jnp.maximum(partners_ref[first + slot], 0) // per
        rows = recv_taps[source].astype(jnp.float32)
        toeplitz_into(partner_toeplitz, slot, rows, chunks, masks)

    def powers_of(rows_ref, matrix, blocks):
        product = jnp.dot(rows_ref[...], matrix, preferred_element_type=jnp.float32)
        result = []
        for window in range(windows):
            real = product[2 * window * blocks : (2 * window + 1) * blocks]
            imag = product[(2 * window + 1) * blocks : (2 * window + 2) * blocks]
            re = real[:, :LANES] - imag[:, LANES:]
            im = real[:, LANES:] + imag[:, :LANES]
            result.append(re * re + im * im)
        return result

    half.collect(chunks)

    @pl.loop(0, per, unroll=4)
    def _(slot):
        values = powers_of(half.blocked, partner_toeplitz[slot], half_blocks)
        planes[slot] = jnp.concatenate(values, axis=0).astype(jnp.bfloat16)

    doubling_row = lax.broadcasted_iota(jnp.int32, (LANES, 2 * LANES), 0)
    doubling_lane = lax.broadcasted_iota(jnp.int32, (LANES, 2 * LANES), 1)
    doubling = (doubling_row == doubling_lane // 2).astype(jnp.bfloat16)

    @pl.loop(0, per, unroll=4)
    def _(slot):
        doubled = jnp.dot(planes[slot], doubling, preferred_element_type=jnp.float32)
        for window in range(windows):
            base = (window * per + slot) * whole_blocks
            part = doubled[window * half_blocks : (window + 1) * half_blocks]
            for side in range(2):
                doubles[pl.ds(base + side, half_blocks, stride=2), :] = part[
                    :, side * LANES : (side + 1) * LANES
                ]

    whole.collect(chunks)
    pitch = per + 1
    live = jnp.full((whole_blocks, LANES), counts_ref[column], jnp.int32)

    @pl.loop(0, per, unroll=2)
    def _(slot):
        values = powers_of(whole.blocked, own_toeplitz[slot], whole_blocks)
        for window in range(windows):
            base = pl.multiple_of((window * per + slot) * whole_blocks, 8)
            total = values[window] + doubles[pl.ds(base, whole_blocks), :]
            rows = pl.ds(window * whole_blocks * pitch + slot, whole_blocks, stride=pitch)
            totals[rows, :] = jnp.where(live > slot, total, 0.0)

    for window in range(windows):
        for block in range(whole_blocks):
            rows = pl.ds((window * whole_blocks + block) * pitch, per)
            out_ref[window, :, pl.ds(block * LANES, LANES)] = totals[rows, :].astype(jnp.bfloat16)

    @pl.loop(1, width)
    def _(step):
        taps_copy(lax.rem(column + step, width)).wait_send()

    half.finish()
    whole.finish()


def body(spectra, half_spectra, kernels, owners, counts, partners):
    width = lax.axis_size("tmpl")
    trials = lax.axis_size("trial")
    group = width * trials // 2
    per, _, taps = kernels.shape
    windows = spectra.shape[0]
    chunks = taps // LANES
    whole_bins = spectra.shape[4] - taps
    whole_blocks = whole_bins // LANES
    half_blocks = (half_spectra.shape[4] - taps) // LANES
    half_hubs = max(1, group * (half_blocks + chunks) // (whole_blocks + half_blocks + 2 * chunks))
    half = Stream(group, windows, half_blocks, chunks, 0, half_hubs)
    whole = Stream(group, windows, whole_blocks, chunks, half.hubs, group - half.hubs)
    plan = (width, trials, per, chunks, half, whole)
    span = (chunks + 1) * LANES
    bf16, f32 = jnp.bfloat16, jnp.float32
    dma = pltpu.SemaphoreType.DMA
    operands = (owners, counts, partners, spectra[:, 0, 0], half_spectra[:, 0, 0], kernels)
    near = (pltpu.SMEM, pltpu.SMEM, pltpu.SMEM, pltpu.VMEM, pltpu.VMEM, pltpu.VMEM)
    hbm = pl.BlockSpec(memory_space=pltpu.HBM)
    tap_rows = -(-2 * chunks // TILE) * TILE * (2 if 2 * chunks % TILE == 0 else 1)
    flops = 4 * per * 2 * span * windows * LANES * (whole_blocks + half_blocks)
    powers = pl.pallas_call(
        functools.partial(kernel, plan),
        out_shape=jax.ShapeDtypeStruct((windows, per, whole_bins), bf16),
        in_specs=[hbm] * 6,
        out_specs=pl.BlockSpec(memory_space=pltpu.VMEM),
        scratch_shapes=[
            *[space(held.shape, held.dtype) for space, held in zip(near, operands)],
            *half.scratch(trials, span),
            *whole.scratch(trials, span),
            pltpu.VMEM((width, tap_rows, LANES), bf16),
            pltpu.VMEM((width, tap_rows, LANES), bf16),
            pltpu.VMEM((per, 2 * chunks, LANES), f32),
            pltpu.VMEM((per, span, 2 * LANES), bf16),
            pltpu.VMEM((per, span, 2 * LANES), bf16),
            pltpu.VMEM((per, windows * half_blocks, LANES), bf16),
            pltpu.VMEM((windows * per * whole_blocks, LANES), f32),
            pltpu.VMEM((windows * whole_blocks * (per + 1), LANES), f32),
            dma((width,)),
            dma((width,)),
            dma((6,)),
        ],
        compiler_params=pltpu.CompilerParams(
            collective_id=0, has_side_effects=True, vmem_limit_bytes=56 * 1024 * 1024
        ),
        cost_estimate=pl.CostEstimate(flops=flops, bytes_accessed=2 * windows * per * whole_bins, transcendentals=0),
    )(*operands)
    return powers[:, None]


def solution(mesh):
    return jax.shard_map(
        body,
        mesh=mesh,
        in_specs=(
            P(None, "trial", "tmpl", None, None),
            P(None, "trial", "tmpl", None, None),
            P("tmpl", None, None),
            P(),
            P(),
            P(),
        ),
        out_specs=P(None, "trial", "tmpl", None),
        check_vma=False,
    )
```

```python
import functools

import jax
import jax.numpy as jnp
from jax import lax
from jax.experimental import pallas as pl
from jax.experimental.pallas import tpu as pltpu
from jax.sharding import PartitionSpec as P

LANES = 128
TILE = 16
MESH = pl.DeviceIdType.MESH


def toeplitz_into(target, slot, chunk_rows, chunks, masks):
    zero = jnp.zeros((TILE, LANES), jnp.bfloat16)
    steps = LANES // TILE
    for part in range(2):
        previous = [zero] * steps
        for number in range(chunks + 1):
            current = [zero] * steps
            if number < chunks:
                row = 2 * number + part
                spread = jnp.broadcast_to(chunk_rows[row : row + 1], (TILE, LANES))
                turned = pltpu.roll(spread, 0, 1, stride=1, stride_axis=0).astype(jnp.bfloat16)
                current = [turned] + [
                    pltpu.roll(turned, step * TILE, 1) for step in range(1, steps)
                ]
            for step in range(steps):
                block = jnp.where(masks[step], current[step], previous[step])
                rows = pl.ds(number * LANES + step * TILE, TILE)
                target[slot, rows, pl.ds(part * LANES, LANES)] = block
            previous = current


SPREAD = 5


class Stream:
    def __init__(self, group, windows, blocks, chunks, first_hub, most_hubs):
        self.group, self.windows, self.blocks, self.first_hub = group, windows, blocks, first_hub
        self.channel_rows = blocks + chunks
        self.window_rows = 2 * self.channel_rows
        self.rows = windows * self.window_rows
        tiles = -(-self.rows // TILE)
        piece_tiles = -(-tiles // most_hubs)
        self.hubs = -(-tiles // piece_tiles)
        self.piece_rows = piece_tiles * TILE
        self.padded = self.hubs * self.piece_rows

    def scratch(self, trials, span):
        bf16, f32, dma = jnp.bfloat16, jnp.float32, pltpu.SemaphoreType.DMA
        return [
            pltpu.VMEM((self.padded, LANES), bf16),
            pltpu.VMEM((self.group, self.piece_rows, LANES), bf16),
            pltpu.VMEM((trials, self.piece_rows, LANES), bf16),
            pltpu.VMEM((trials, self.piece_rows, LANES), bf16),
            pltpu.VMEM((trials, self.piece_rows, LANES), bf16),
            pltpu.VMEM((self.padded, LANES), bf16),
            pltpu.VMEM((self.padded, LANES), f32),
            pltpu.VMEM((2 * self.windows * self.blocks, span), bf16),
            dma((self.hubs,)),
            dma((self.group,)),
            dma((2,)),
            dma((self.group,)),
            dma((self.hubs,)),
        ]

    def bind(self, refs, trials, width, trial, me):
        (
            self.stored,
            self.candidates,
            self.chosen,
            self.across,
            self.settled,
            self.gathered,
            self.widened,
            self.blocked,
            self.piece_send,
            self.piece_recv,
            self.swap_sem,
            self.chosen_send,
            self.chosen_recv,
        ) = refs
        self.trials, self.width, self.trial, self.me = trials, width, trial, me
        self.my_group = me // self.group
        self.local = lax.rem(me, self.group)
        back = pow(SPREAD, -1, self.group)
        turn = lax.rem(self.local * back + self.group - self.first_hub, self.group)
        self.is_hub = turn < self.hubs
        self.my_hub = jnp.minimum(turn, self.hubs - 1)
        self.my_rows = self.piece(self.my_hub)

    def hub_local(self, hub):
        return lax.rem((hub + self.first_hub) * SPREAD, self.group)

    def piece(self, hub):
        return pl.ds(pl.multiple_of(hub * self.piece_rows, TILE), self.piece_rows)

    def place(self, flat):
        return (lax.rem(flat, self.trials), flat // self.trials)

    def near(self, local):
        return self.place(self.my_group * self.group + local)

    def lay_out(self, held):
        for window in range(self.windows):
            for number in range(self.channel_rows):
                rows = pl.ds(window * self.window_rows + number, 2, stride=self.channel_rows)
                lanes = pl.ds(number * LANES, LANES)
                self.widened[rows, :] = held[window, :, lanes].astype(jnp.float32)
        rest = self.padded - self.rows
        if rest:
            self.widened[pl.ds(self.rows, rest), :] = jnp.zeros((rest, LANES), jnp.float32)
        self.stored[...] = self.widened[...].astype(jnp.bfloat16)

    def piece_copy(self, hub):
        return pltpu.make_async_remote_copy(
            src_ref=self.stored.at[self.piece(hub)],
            dst_ref=self.candidates.at[self.local],
            send_sem=self.piece_send.at[hub],
            recv_sem=self.piece_recv.at[self.local],
            device_id=self.near(self.hub_local(hub)),
            device_id_type=MESH,
        )

    def each_other_hub(self, act):
        @pl.loop(0, self.hubs)
        def _(step):
            hub = lax.rem(self.local + step, self.hubs)

            @pl.when(self.hub_local(hub) != self.local)
            def _():
                act(hub)

    def each_other_device(self, act):
        @pl.loop(1, self.group)
        def _(step):
            act(lax.rem(self.local + step, self.group))

    def scatter(self):
        self.each_other_hub(lambda hub: self.piece_copy(hub).start())

        @pl.when(self.is_hub)
        def _():
            self.candidates[self.local] = self.stored[self.my_rows, :]

    def chosen_copy(self, target):
        return pltpu.make_async_remote_copy(
            src_ref=self.settled.at[lax.rem(target, self.trials)],
            dst_ref=self.gathered.at[self.my_rows],
            send_sem=self.chosen_send.at[target],
            recv_sem=self.chosen_recv.at[self.my_hub],
            device_id=self.near(target),
            device_id_type=MESH,
        )

    def arrival(self, ref, send_sem, recv_sem, device):
        return pltpu.make_async_remote_copy(
            src_ref=ref,
            dst_ref=ref,
            send_sem=send_sem,
            recv_sem=recv_sem,
            device_id=self.near(device),
            device_id_type=MESH,
        )

    def by_window(self, take):
        number = lax.broadcasted_iota(jnp.int32, (self.piece_rows, LANES), 0)
        number = number + self.my_hub * self.piece_rows
        kept = take(0)
        for window in range(1, self.windows):
            kept = jnp.where(number >= window * self.window_rows, take(window), kept)
        return kept.astype(jnp.bfloat16)

    def flat_owner(self, owners_ref, window, which):
        owner = owners_ref[window, which]
        return lax.rem(owner, self.width) * self.trials + owner // self.width

    def swap_copy(self):
        return pltpu.make_async_remote_copy(
            src_ref=self.chosen,
            dst_ref=self.across,
            send_sem=self.swap_sem.at[0],
            recv_sem=self.swap_sem.at[1],
            device_id=self.place(lax.rem(self.me + self.group, 2 * self.group)),
            device_id_type=MESH,
        )

    def choose(self, owners_ref):
        @pl.when(self.is_hub)
        def _():
            self.each_other_device(
                lambda other: self.arrival(
                    self.candidates.at[other],
                    self.piece_send.at[0],
                    self.piece_recv.at[other],
                    other,
                ).wait_recv()
            )
            for which in range(self.trials):

                def take(window):
                    source = lax.rem(self.flat_owner(owners_ref, window, which), self.group)
                    return self.candidates[source].astype(jnp.float32)

                self.chosen[which] = self.by_window(take)
            self.swap_copy().start()

    def settle(self, owners_ref):
        @pl.when(self.is_hub)
        def _():
            self.swap_copy().wait()
            shape = (self.piece_rows, LANES)
            for which in range(self.trials):
                mine = self.chosen[which].astype(jnp.float32)
                theirs = self.across[which].astype(jnp.float32)

                def take(window):
                    holder = self.flat_owner(owners_ref, window, which) // self.group
                    return jnp.where(jnp.full(shape, holder) == self.my_group, mine, theirs)

                self.settled[which] = self.by_window(take)
            self.each_other_device(lambda target: self.chosen_copy(target).start())
            self.gathered[self.my_rows, :] = self.settled[self.trial]

    def collect(self, chunks):
        self.each_other_hub(
            lambda hub: self.arrival(
                self.gathered.at[self.piece(hub)],
                self.chosen_send.at[0],
                self.chosen_recv.at[hub],
                self.hub_local(hub),
            ).wait_recv()
        )
        self.widened[...] = self.gathered[...].astype(jnp.float32)
        for pair in range(2 * self.windows):
            for number in range(chunks + 1):
                begin = pair * self.channel_rows + number
                rows = pl.ds(pair * self.blocks, self.blocks)
                self.blocked[rows, pl.ds(number * LANES, LANES)] = self.widened[
                    pl.ds(begin, self.blocks), :
                ].astype(jnp.bfloat16)

    def finish(self):
        self.each_other_hub(lambda hub: self.piece_copy(hub).wait_send())

        @pl.when(self.is_hub)
        def _():
            self.each_other_device(lambda target: self.chosen_copy(target).wait_send())


def kernel(plan, *refs):
    width, trials, per, chunks, half, whole = plan
    operands, out_ref, refs = refs[:6], refs[6], refs[7:]
    locals_, refs = refs[:6], refs[6:]
    half_refs, whole_refs, refs = refs[:13], refs[13:26], refs[26:]
    owners_ref, counts_ref, partners_ref, taps_ref, spectra_ref, halved_ref = locals_
    (
        send_taps,
        recv_taps,
        flipped,
        own_toeplitz,
        partner_toeplitz,
        planes,
        doubles,
        totals,
        taps_send,
        taps_recv,
        local_sem,
    ) = refs
    windows, whole_blocks, half_blocks = whole.windows, whole.blocks, half.blocks
    trial = lax.axis_index("trial")
    column = lax.axis_index("tmpl")
    me = column * trials + trial
    half.bind(half_refs, trials, width, trial, me)
    whole.bind(whole_refs, trials, width, trial, me)

    local_copies = [
        pltpu.make_async_copy(operands[number], locals_[number], local_sem.at[number])
        for number in range(6)
    ]
    for copy in reversed(local_copies):
        copy.start()

    barrier = pltpu.get_barrier_semaphore()

    def greet(place):
        pl.semaphore_signal(barrier, inc=1, device_id=place, device_id_type=MESH)

    far_column = (1 - me // whole.group) * (width // 2)
    whole.each_other_device(lambda other: greet(whole.near(other)))

    @pl.loop(0, width // 2)
    def _(step):
        greet((trial, far_column + step))

    local_copies[5].wait()
    half.lay_out(halved_ref)
    pl.semaphore_wait(barrier, whole.group - 1 + width // 2)
    half.scatter()
    local_copies[4].wait()
    whole.lay_out(spectra_ref)
    whole.scatter()
    for copy in local_copies[:4]:
        copy.wait()

    row_number = lax.broadcasted_iota(jnp.int32, (LANES, LANES), 0)
    lane_number = lax.broadcasted_iota(jnp.int32, (LANES, LANES), 1)
    masks = [
        row_number[step * TILE : (step + 1) * TILE] >= lane_number[:TILE]
        for step in range(LANES // TILE)
    ]
    flip = ((row_number + lane_number) % LANES == 0).astype(jnp.bfloat16)
    for number in range(chunks):
        held = taps_ref[:, :, pl.ds(number * LANES, LANES)].astype(jnp.float32)
        held = held.reshape(2 * per, LANES).astype(jnp.bfloat16)
        turned = jnp.dot(held, flip, preferred_element_type=jnp.float32)
        flipped[:, pl.ds(2 * number, 2), :] = turned.reshape(per, 2, LANES)

    first = column * per

    @pl.loop(0, width)
    def _(receiver):
        slot = jnp.int32(0)
        for position in range(per):
            named = partners_ref[receiver * per + position] - first
            slot = jnp.where((named >= 0) & (named < per), named, slot)
        rows = flipped[slot]
        send_taps[receiver] = jnp.concatenate([rows, rows], axis=0).astype(jnp.bfloat16)

    def taps_copy(receiver):
        return pltpu.make_async_remote_copy(
            src_ref=send_taps.at[receiver],
            dst_ref=recv_taps.at[column],
            send_sem=taps_send.at[receiver],
            recv_sem=taps_recv.at[column],
            device_id=(trial, receiver),
            device_id_type=MESH,
        )

    @pl.loop(1, width)
    def _(step):
        taps_copy(lax.rem(column + step, width)).start()

    recv_taps[column] = send_taps[column]

    def build_own(begin, end):
        @pl.loop(begin, end, unroll=2)
        def _(slot):
            toeplitz_into(own_toeplitz, slot, flipped[slot], chunks, masks)

    build_own(0, per // 2)
    half.choose(owners_ref)
    build_own(per // 2, 3 * per // 4)
    half.settle(owners_ref)
    whole.choose(owners_ref)
    build_own(3 * per // 4, per)
    whole.settle(owners_ref)

    @pl.loop(1, width)
    def _(step):
        other = lax.rem(column + step, width)
        pltpu.make_async_remote_copy(
            src_ref=recv_taps.at[other],
            dst_ref=recv_taps.at[other],
            send_sem=taps_send.at[0],
            recv_sem=taps_recv.at[other],
            device_id=(trial, other),
            device_id_type=MESH,
        ).wait_recv()

    @pl.loop(0, per, unroll=2)
    def _(slot):
        source = jnp.maximum(partners_ref[first + slot], 0) // per
        rows = recv_taps[source].astype(jnp.float32)
        toeplitz_into(partner_toeplitz, slot, rows, chunks, masks)

    def powers_of(rows_ref, matrix, blocks):
        product = jnp.dot(rows_ref[...], matrix, preferred_element_type=jnp.float32)
        result = []
        for window in range(windows):
            real = product[2 * window * blocks : (2 * window + 1) * blocks]
            imag = product[(2 * window + 1) * blocks : (2 * window + 2) * blocks]
            re = real[:, :LANES] - imag[:, LANES:]
            im = real[:, LANES:] + imag[:, :LANES]
            result.append(re * re + im * im)
        return result

    half.collect(chunks)

    @pl.loop(0, per, unroll=4)
    def _(slot):
        values = powers_of(half.blocked, partner_toeplitz[slot], half_blocks)
        planes[slot] = jnp.concatenate(values, axis=0).astype(jnp.bfloat16)

    doubling_row = lax.broadcasted_iota(jnp.int32, (LANES, 2 * LANES), 0)
    doubling_lane = lax.broadcasted_iota(jnp.int32, (LANES, 2 * LANES), 1)
    doubling = (doubling_row == doubling_lane // 2).astype(jnp.bfloat16)

    @pl.loop(0, per, unroll=4)
    def _(slot):
        doubled = jnp.dot(planes[slot], doubling, preferred_element_type=jnp.float32)
        for window in range(windows):
            base = (window * per + slot) * whole_blocks
            part = doubled[window * half_blocks : (window + 1) * half_blocks]
            for side in range(2):
                doubles[pl.ds(base + side, half_blocks, stride=2), :] = part[
                    :, side * LANES : (side + 1) * LANES
                ]

    whole.collect(chunks)
    pitch = per + 1
    live = jnp.full((whole_blocks, LANES), counts_ref[column], jnp.int32)

    @pl.loop(0, per, unroll=2)
    def _(slot):
        values = powers_of(whole.blocked, own_toeplitz[slot], whole_blocks)
        for window in range(windows):
            base = pl.multiple_of((window * per + slot) * whole_blocks, 8)
            total = values[window] + doubles[pl.ds(base, whole_blocks), :]
            rows = pl.ds(window * whole_blocks * pitch + slot, whole_blocks, stride=pitch)
            totals[rows, :] = jnp.where(live > slot, total, 0.0)

    for window in range(windows):
        for block in range(whole_blocks):
            rows = pl.ds((window * whole_blocks + block) * pitch, per)
            out_ref[window, :, pl.ds(block * LANES, LANES)] = totals[rows, :].astype(jnp.bfloat16)

    @pl.loop(1, width)
    def _(step):
        taps_copy(lax.rem(column + step, width)).wait_send()

    half.finish()
    whole.finish()


def body(spectra, half_spectra, kernels, owners, counts, partners):
    width = lax.axis_size("tmpl")
    trials = lax.axis_size("trial")
    group = width * trials // 2
    per, _, taps = kernels.shape
    windows = spectra.shape[0]
    chunks = taps // LANES
    whole_bins = spectra.shape[4] - taps
    whole_blocks = whole_bins // LANES
    half_blocks = (half_spectra.shape[4] - taps) // LANES
    half_hubs = max(1, group * (half_blocks + chunks) // (whole_blocks + half_blocks + 2 * chunks))
    half = Stream(group, windows, half_blocks, chunks, 0, half_hubs)
    whole = Stream(group, windows, whole_blocks, chunks, half.hubs, group - half.hubs)
    plan = (width, trials, per, chunks, half, whole)
    span = (chunks + 1) * LANES
    bf16, f32 = jnp.bfloat16, jnp.float32
    dma = pltpu.SemaphoreType.DMA
    operands = (owners, counts, partners, kernels, spectra[:, 0, 0], half_spectra[:, 0, 0])
    operands = tuple(pltpu.with_memory_space_constraint(held, pltpu.HBM) for held in operands)
    near = (pltpu.SMEM, pltpu.SMEM, pltpu.SMEM, pltpu.VMEM, pltpu.VMEM, pltpu.VMEM)
    hbm = pl.BlockSpec(memory_space=pltpu.HBM)
    tap_rows = -(-2 * chunks // TILE) * TILE * (2 if 2 * chunks % TILE == 0 else 1)
    flops = 4 * per * 2 * span * windows * LANES * (whole_blocks + half_blocks)
    powers = pl.pallas_call(
        functools.partial(kernel, plan),
        out_shape=jax.ShapeDtypeStruct((windows, per, whole_bins), bf16),
        in_specs=[hbm] * 6,
        out_specs=pl.BlockSpec(memory_space=pltpu.VMEM),
        scratch_shapes=[
            *[space(held.shape, held.dtype) for space, held in zip(near, operands)],
            *half.scratch(trials, span),
            *whole.scratch(trials, span),
            pltpu.VMEM((width, tap_rows, LANES), bf16),
            pltpu.VMEM((width, tap_rows, LANES), bf16),
            pltpu.VMEM((per, 2 * chunks, LANES), f32),
            pltpu.VMEM((per, span, 2 * LANES), bf16),
            pltpu.VMEM((per, span, 2 * LANES), bf16),
            pltpu.VMEM((per, windows * half_blocks, LANES), bf16),
            pltpu.VMEM((windows * per * whole_blocks, LANES), f32),
            pltpu.VMEM((windows * whole_blocks * (per + 1), LANES), f32),
            dma((width,)),
            dma((width,)),
            dma((6,)),
        ],
        compiler_params=pltpu.CompilerParams(
            collective_id=0, has_side_effects=True, vmem_limit_bytes=48 * 1024 * 1024
        ),
        cost_estimate=pl.CostEstimate(flops=flops, bytes_accessed=2 * windows * per * whole_bins, transcendentals=0),
    )(*operands)
    return powers[:, None]


def solution(mesh):
    return jax.shard_map(
        body,
        mesh=mesh,
        in_specs=(
            P(None, "trial", "tmpl", None, None),
            P(None, "trial", "tmpl", None, None),
            P("tmpl", None, None),
            P(),
            P(),
            P(),
        ),
        out_specs=P(None, "trial", "tmpl", None),
        check_vma=False,
    )
```

```python
import functools

import jax
import jax.numpy as jnp
from jax import lax
from jax.experimental import pallas as pl
from jax.experimental.pallas import tpu as pltpu
from jax.sharding import PartitionSpec as P

LANES = 128
TILE = 16
MESH = pl.DeviceIdType.MESH


def toeplitz_into(target, slot, chunk_rows, chunks, masks):
    zero = jnp.zeros((TILE, LANES), jnp.bfloat16)
    steps = LANES // TILE
    for part in range(2):
        previous = [zero] * steps
        for number in range(chunks + 1):
            current = [zero] * steps
            if number < chunks:
                row = 2 * number + part
                spread = jnp.broadcast_to(chunk_rows[row : row + 1], (TILE, LANES))
                turned = pltpu.roll(spread, 0, 1, stride=1, stride_axis=0).astype(jnp.bfloat16)
                current = [turned] + [
                    pltpu.roll(turned, step * TILE, 1) for step in range(1, steps)
                ]
            for step in range(steps):
                block = jnp.where(masks[step], current[step], previous[step])
                rows = pl.ds(number * LANES + step * TILE, TILE)
                target[slot, rows, pl.ds(part * LANES, LANES)] = block
            previous = current


SPREAD = 5


class Stream:
    def __init__(self, group, windows, blocks, chunks, first_hub, most_hubs):
        self.group, self.windows, self.blocks, self.first_hub = group, windows, blocks, first_hub
        self.channel_rows = blocks + chunks
        self.window_rows = 2 * self.channel_rows
        self.rows = windows * self.window_rows
        tiles = -(-self.rows // TILE)
        piece_tiles = -(-tiles // most_hubs)
        self.hubs = -(-tiles // piece_tiles)
        self.piece_rows = piece_tiles * TILE
        self.padded = self.hubs * self.piece_rows

    def scratch(self, trials, span):
        bf16, f32, dma = jnp.bfloat16, jnp.float32, pltpu.SemaphoreType.DMA
        return [
            pltpu.VMEM((self.padded, LANES), bf16),
            pltpu.VMEM((self.group, self.piece_rows, LANES), bf16),
            pltpu.VMEM((trials, self.piece_rows, LANES), bf16),
            pltpu.VMEM((trials, self.piece_rows, LANES), bf16),
            pltpu.VMEM((trials, self.piece_rows, LANES), bf16),
            pltpu.VMEM((self.padded, LANES), bf16),
            pltpu.VMEM((self.padded, LANES), f32),
            pltpu.VMEM((2 * self.windows * self.blocks, span), bf16),
            dma((self.hubs,)),
            dma((self.group,)),
            dma((2,)),
            dma((self.group,)),
            dma((self.hubs,)),
        ]

    def bind(self, refs, trials, width, trial, me):
        (
            self.stored,
            self.candidates,
            self.chosen,
            self.across,
            self.settled,
            self.gathered,
            self.widened,
            self.blocked,
            self.piece_send,
            self.piece_recv,
            self.swap_sem,
            self.chosen_send,
            self.chosen_recv,
        ) = refs
        self.trials, self.width, self.trial, self.me = trials, width, trial, me
        self.my_group = me // self.group
        self.local = lax.rem(me, self.group)
        back = pow(SPREAD, -1, self.group)
        turn = lax.rem(self.local * back + self.group - self.first_hub, self.group)
        self.is_hub = turn < self.hubs
        self.my_hub = jnp.minimum(turn, self.hubs - 1)
        self.my_rows = self.piece(self.my_hub)

    def hub_local(self, hub):
        return lax.rem((hub + self.first_hub) * SPREAD, self.group)

    def piece(self, hub):
        return pl.ds(pl.multiple_of(hub * self.piece_rows, TILE), self.piece_rows)

    def place(self, flat):
        return (lax.rem(flat, self.trials), flat // self.trials)

    def near(self, local):
        return self.place(self.my_group * self.group + local)

    def lay_out(self, held):
        for window in range(self.windows):


            @pl.loop(0, self.channel_rows, unroll=4)
            def _(number):
                rows = pl.ds(window * self.window_rows + number, 2, stride=self.channel_rows)
                lanes = pl.ds(pl.multiple_of(number * LANES, LANES), LANES)
                self.widened[rows, :] = held[window, :, lanes].astype(jnp.float32)
        rest = self.padded - self.rows
        if rest:
            self.widened[pl.ds(self.rows, rest), :] = jnp.zeros((rest, LANES), jnp.float32)
        self.stored[...] = self.widened[...].astype(jnp.bfloat16)

    def piece_copy(self, hub):
        return pltpu.make_async_remote_copy(
            src_ref=self.stored.at[self.piece(hub)],
            dst_ref=self.candidates.at[self.local],
            send_sem=self.piece_send.at[hub],
            recv_sem=self.piece_recv.at[self.local],
            device_id=self.near(self.hub_local(hub)),
            device_id_type=MESH,
        )

    def each_other_hub(self, act):
        @pl.loop(0, self.hubs)
        def _(step):
            hub = lax.rem(self.local + step, self.hubs)

            @pl.when(self.hub_local(hub) != self.local)
            def _():
                act(hub)

    def each_other_device(self, act):
        @pl.loop(1, self.group)
        def _(step):
            act(lax.rem(self.local + step, self.group))

    def scatter(self):
        self.each_other_hub(lambda hub: self.piece_copy(hub).start())

        @pl.when(self.is_hub)
        def _():
            self.candidates[self.local] = self.stored[self.my_rows, :]

    def chosen_copy(self, target):
        return pltpu.make_async_remote_copy(
            src_ref=self.settled.at[lax.rem(target, self.trials)],
            dst_ref=self.gathered.at[self.my_rows],
            send_sem=self.chosen_send.at[target],
            recv_sem=self.chosen_recv.at[self.my_hub],
            device_id=self.near(target),
            device_id_type=MESH,
        )

    def arrival(self, ref, send_sem, recv_sem, device):
        return pltpu.make_async_remote_copy(
            src_ref=ref,
            dst_ref=ref,
            send_sem=send_sem,
            recv_sem=recv_sem,
            device_id=self.near(device),
            device_id_type=MESH,
        )

    def by_window(self, take):
        number = lax.broadcasted_iota(jnp.int32, (self.piece_rows, LANES), 0)
        number = number + self.my_hub * self.piece_rows
        kept = take(0)
        for window in range(1, self.windows):
            kept = jnp.where(number >= window * self.window_rows, take(window), kept)
        return kept.astype(jnp.bfloat16)

    def flat_owner(self, owners_ref, window, which):
        owner = owners_ref[window, which]
        return lax.rem(owner, self.width) * self.trials + owner // self.width

    def swap_copy(self):
        return pltpu.make_async_remote_copy(
            src_ref=self.chosen,
            dst_ref=self.across,
            send_sem=self.swap_sem.at[0],
            recv_sem=self.swap_sem.at[1],
            device_id=self.place(lax.rem(self.me + self.group, 2 * self.group)),
            device_id_type=MESH,
        )

    def choose(self, owners_ref):
        @pl.when(self.is_hub)
        def _():
            self.each_other_device(
                lambda other: self.arrival(
                    self.candidates.at[other],
                    self.piece_send.at[0],
                    self.piece_recv.at[other],
                    other,
                ).wait_recv()
            )
            for which in range(self.trials):

                def take(window):
                    source = lax.rem(self.flat_owner(owners_ref, window, which), self.group)
                    return self.candidates[source].astype(jnp.float32)

                self.chosen[which] = self.by_window(take)
            self.swap_copy().start()

    def settle(self, owners_ref):
        @pl.when(self.is_hub)
        def _():
            self.swap_copy().wait()
            shape = (self.piece_rows, LANES)
            for which in range(self.trials):
                mine = self.chosen[which].astype(jnp.float32)
                theirs = self.across[which].astype(jnp.float32)

                def take(window):
                    holder = self.flat_owner(owners_ref, window, which) // self.group
                    return jnp.where(jnp.full(shape, holder) == self.my_group, mine, theirs)

                self.settled[which] = self.by_window(take)
            self.each_other_device(lambda target: self.chosen_copy(target).start())
            self.gathered[self.my_rows, :] = self.settled[self.trial]

    def collect(self, chunks):
        self.each_other_hub(
            lambda hub: self.arrival(
                self.gathered.at[self.piece(hub)],
                self.chosen_send.at[0],
                self.chosen_recv.at[hub],
                self.hub_local(hub),
            ).wait_recv()
        )
        self.widened[...] = self.gathered[...].astype(jnp.float32)
        for pair in range(2 * self.windows):
            for number in range(chunks + 1):
                begin = pair * self.channel_rows + number
                rows = pl.ds(pair * self.blocks, self.blocks)
                self.blocked[rows, pl.ds(number * LANES, LANES)] = self.widened[
                    pl.ds(begin, self.blocks), :
                ].astype(jnp.bfloat16)

    def finish(self):
        self.each_other_hub(lambda hub: self.piece_copy(hub).wait_send())

        @pl.when(self.is_hub)
        def _():
            self.each_other_device(lambda target: self.chosen_copy(target).wait_send())


def kernel(plan, *refs):
    width, trials, per, chunks, half, whole = plan
    operands, out_ref, refs = refs[:6], refs[6], refs[7:]
    locals_, refs = refs[:6], refs[6:]
    half_refs, whole_refs, refs = refs[:13], refs[13:26], refs[26:]
    owners_ref, counts_ref, partners_ref, taps_ref, spectra_ref, halved_ref = locals_
    (
        send_taps,
        recv_taps,
        flipped,
        own_toeplitz,
        partner_toeplitz,
        planes,
        doubles,
        totals,
        taps_send,
        taps_recv,
        local_sem,
    ) = refs
    windows, whole_blocks, half_blocks = whole.windows, whole.blocks, half.blocks
    trial = lax.axis_index("trial")
    column = lax.axis_index("tmpl")
    me = column * trials + trial
    half.bind(half_refs, trials, width, trial, me)
    whole.bind(whole_refs, trials, width, trial, me)

    local_copies = [
        pltpu.make_async_copy(operands[number], locals_[number], local_sem.at[number])
        for number in range(6)
    ]
    for copy in reversed(local_copies):
        copy.start()

    barrier = pltpu.get_barrier_semaphore()

    def greet(place):
        pl.semaphore_signal(barrier, inc=1, device_id=place, device_id_type=MESH)

    far_column = (1 - me // whole.group) * (width // 2)
    whole.each_other_device(lambda other: greet(whole.near(other)))

    @pl.loop(0, width // 2)
    def _(step):
        greet((trial, far_column + step))

    local_copies[5].wait()
    half.lay_out(halved_ref)
    pl.semaphore_wait(barrier, whole.group - 1 + width // 2)
    half.scatter()
    local_copies[4].wait()
    whole.lay_out(spectra_ref)
    whole.scatter()
    for copy in local_copies[:4]:
        copy.wait()

    row_number = lax.broadcasted_iota(jnp.int32, (LANES, LANES), 0)
    lane_number = lax.broadcasted_iota(jnp.int32, (LANES, LANES), 1)
    masks = [
        row_number[step * TILE : (step + 1) * TILE] >= lane_number[:TILE]
        for step in range(LANES // TILE)
    ]
    flip = ((row_number + lane_number) % LANES == 0).astype(jnp.bfloat16)
    for number in range(chunks):
        held = taps_ref[:, :, pl.ds(number * LANES, LANES)].astype(jnp.float32)
        held = held.reshape(2 * per, LANES).astype(jnp.bfloat16)
        turned = jnp.dot(held, flip, preferred_element_type=jnp.float32)
        flipped[:, pl.ds(2 * number, 2), :] = turned.reshape(per, 2, LANES)

    first = column * per

    @pl.loop(0, width)
    def _(receiver):
        slot = jnp.int32(0)
        for position in range(per):
            named = partners_ref[receiver * per + position] - first
            slot = jnp.where((named >= 0) & (named < per), named, slot)
        rows = flipped[slot]
        send_taps[receiver] = jnp.concatenate([rows, rows], axis=0).astype(jnp.bfloat16)

    def taps_copy(receiver):
        return pltpu.make_async_remote_copy(
            src_ref=send_taps.at[receiver],
            dst_ref=recv_taps.at[column],
            send_sem=taps_send.at[receiver],
            recv_sem=taps_recv.at[column],
            device_id=(trial, receiver),
            device_id_type=MESH,
        )

    @pl.loop(1, width)
    def _(step):
        taps_copy(lax.rem(column + step, width)).start()

    recv_taps[column] = send_taps[column]

    def build_own(begin, end):
        @pl.loop(begin, end, unroll=2)
        def _(slot):
            toeplitz_into(own_toeplitz, slot, flipped[slot], chunks, masks)

    build_own(0, per // 2)
    half.choose(owners_ref)
    build_own(per // 2, 3 * per // 4)
    half.settle(owners_ref)
    whole.choose(owners_ref)
    build_own(3 * per // 4, per)
    whole.settle(owners_ref)

    @pl.loop(1, width)
    def _(step):
        other = lax.rem(column + step, width)
        pltpu.make_async_remote_copy(
            src_ref=recv_taps.at[other],
            dst_ref=recv_taps.at[other],
            send_sem=taps_send.at[0],
            recv_sem=taps_recv.at[other],
            device_id=(trial, other),
            device_id_type=MESH,
        ).wait_recv()

    @pl.loop(0, per, unroll=2)
    def _(slot):
        source = jnp.maximum(partners_ref[first + slot], 0) // per
        rows = recv_taps[source].astype(jnp.float32)
        toeplitz_into(partner_toeplitz, slot, rows, chunks, masks)

    def powers_of(rows_ref, matrix, blocks):
        product = jnp.dot(rows_ref[...], matrix, preferred_element_type=jnp.float32)
        result = []
        for window in range(windows):
            real = product[2 * window * blocks : (2 * window + 1) * blocks]
            imag = product[(2 * window + 1) * blocks : (2 * window + 2) * blocks]
            re = real[:, :LANES] - imag[:, LANES:]
            im = real[:, LANES:] + imag[:, :LANES]
            result.append(re * re + im * im)
        return result

    half.collect(chunks)

    @pl.loop(0, per, unroll=4)
    def _(slot):
        values = powers_of(half.blocked, partner_toeplitz[slot], half_blocks)
        planes[slot] = jnp.concatenate(values, axis=0).astype(jnp.bfloat16)

    doubling_row = lax.broadcasted_iota(jnp.int32, (LANES, 2 * LANES), 0)
    doubling_lane = lax.broadcasted_iota(jnp.int32, (LANES, 2 * LANES), 1)
    doubling = (doubling_row == doubling_lane // 2).astype(jnp.bfloat16)

    @pl.loop(0, per, unroll=4)
    def _(slot):
        doubled = jnp.dot(planes[slot], doubling, preferred_element_type=jnp.float32)
        for window in range(windows):
            base = (window * per + slot) * whole_blocks
            part = doubled[window * half_blocks : (window + 1) * half_blocks]
            for side in range(2):
                doubles[pl.ds(base + side, half_blocks, stride=2), :] = part[
                    :, side * LANES : (side + 1) * LANES
                ]

    whole.collect(chunks)
    pitch = per + 1
    live = jnp.full((whole_blocks, LANES), counts_ref[column], jnp.int32)

    @pl.loop(0, per, unroll=2)
    def _(slot):
        values = powers_of(whole.blocked, own_toeplitz[slot], whole_blocks)
        for window in range(windows):
            base = pl.multiple_of((window * per + slot) * whole_blocks, 8)
            total = values[window] + doubles[pl.ds(base, whole_blocks), :]
            rows = pl.ds(window * whole_blocks * pitch + slot, whole_blocks, stride=pitch)
            totals[rows, :] = jnp.where(live > slot, total, 0.0)

    for window in range(windows):

        @pl.loop(0, whole_blocks, unroll=8)
        def _(block):
            rows = pl.ds((window * whole_blocks + block) * pitch, per)
            lanes = pl.ds(pl.multiple_of(block * LANES, LANES), LANES)
            out_ref[window, :, lanes] = totals[rows, :].astype(jnp.bfloat16)

    @pl.loop(1, width)
    def _(step):
        taps_copy(lax.rem(column + step, width)).wait_send()

    half.finish()
    whole.finish()


def body(spectra, half_spectra, kernels, owners, counts, partners):
    width = lax.axis_size("tmpl")
    trials = lax.axis_size("trial")
    group = width * trials // 2
    per, _, taps = kernels.shape
    windows = spectra.shape[0]
    chunks = taps // LANES
    whole_bins = spectra.shape[4] - taps
    whole_blocks = whole_bins // LANES
    half_blocks = (half_spectra.shape[4] - taps) // LANES
    half_hubs = max(1, group * (half_blocks + chunks) // (whole_blocks + half_blocks + 2 * chunks))
    half = Stream(group, windows, half_blocks, chunks, 0, half_hubs)
    whole = Stream(group, windows, whole_blocks, chunks, half.hubs, group - half.hubs)
    plan = (width, trials, per, chunks, half, whole)
    span = (chunks + 1) * LANES
    bf16, f32 = jnp.bfloat16, jnp.float32
    dma = pltpu.SemaphoreType.DMA
    operands = (owners, counts, partners, kernels, spectra[:, 0, 0], half_spectra[:, 0, 0])
    operands = tuple(pltpu.with_memory_space_constraint(held, pltpu.HBM) for held in operands)
    near = (pltpu.SMEM, pltpu.SMEM, pltpu.SMEM, pltpu.VMEM, pltpu.VMEM, pltpu.VMEM)
    hbm = pl.BlockSpec(memory_space=pltpu.HBM)
    tap_rows = -(-2 * chunks // TILE) * TILE * (2 if 2 * chunks % TILE == 0 else 1)
    flops = 4 * per * 2 * span * windows * LANES * (whole_blocks + half_blocks)
    powers = pl.pallas_call(
        functools.partial(kernel, plan),
        out_shape=jax.ShapeDtypeStruct((windows, per, whole_bins), bf16),
        in_specs=[hbm] * 6,
        out_specs=pl.BlockSpec(memory_space=pltpu.VMEM),
        scratch_shapes=[
            *[space(held.shape, held.dtype) for space, held in zip(near, operands)],
            *half.scratch(trials, span),
            *whole.scratch(trials, span),
            pltpu.VMEM((width, tap_rows, LANES), bf16),
            pltpu.VMEM((width, tap_rows, LANES), bf16),
            pltpu.VMEM((per, 2 * chunks, LANES), f32),
            pltpu.VMEM((per, span, 2 * LANES), bf16),
            pltpu.VMEM((per, span, 2 * LANES), bf16),
            pltpu.VMEM((per, windows * half_blocks, LANES), bf16),
            pltpu.VMEM((windows * per * whole_blocks, LANES), f32),
            pltpu.VMEM((windows * whole_blocks * (per + 1), LANES), f32),
            dma((width,)),
            dma((width,)),
            dma((6,)),
        ],
        compiler_params=pltpu.CompilerParams(
            collective_id=0, has_side_effects=True, vmem_limit_bytes=48 * 1024 * 1024
        ),
        cost_estimate=pl.CostEstimate(flops=flops, bytes_accessed=2 * windows * per * whole_bins, transcendentals=0),
    )(*operands)
    return powers[:, None]


def solution(mesh):
    return jax.shard_map(
        body,
        mesh=mesh,
        in_specs=(
            P(None, "trial", "tmpl", None, None),
            P(None, "trial", "tmpl", None, None),
            P("tmpl", None, None),
            P(),
            P(),
            P(),
        ),
        out_specs=P(None, "trial", "tmpl", None),
        check_vma=False,
    )
```

```python
import functools

import jax
import jax.numpy as jnp
from jax import lax
from jax.experimental import pallas as pl
from jax.experimental.pallas import tpu as pltpu
from jax.sharding import PartitionSpec as P

LANES = 128
TILE = 16
MESH = pl.DeviceIdType.MESH


def toeplitz_into(target, slot, chunk_rows, chunks, masks):
    zero = jnp.zeros((TILE, LANES), jnp.bfloat16)
    steps = LANES // TILE
    for part in range(2):
        previous = [zero] * steps
        for number in range(chunks + 1):
            current = [zero] * steps
            if number < chunks:
                row = 2 * number + part
                spread = jnp.broadcast_to(chunk_rows[row : row + 1], (TILE, LANES))
                turned = pltpu.roll(spread, 0, 1, stride=1, stride_axis=0).astype(jnp.bfloat16)
                current = [turned] + [
                    pltpu.roll(turned, step * TILE, 1) for step in range(1, steps)
                ]
            for step in range(steps):
                block = jnp.where(masks[step], current[step], previous[step])
                rows = pl.ds(number * LANES + step * TILE, TILE)
                target[slot, rows, pl.ds(part * LANES, LANES)] = block
            previous = current


SPREAD = 5


class Stream:
    def __init__(self, group, windows, blocks, chunks, first_hub, most_hubs):
        self.group, self.windows, self.blocks, self.first_hub = group, windows, blocks, first_hub
        self.channel_rows = blocks + chunks
        self.window_rows = 2 * self.channel_rows
        self.rows = windows * self.window_rows
        tiles = -(-self.rows // TILE)
        piece_tiles = -(-tiles // most_hubs)
        self.hubs = -(-tiles // piece_tiles)
        self.piece_rows = piece_tiles * TILE
        self.padded = self.hubs * self.piece_rows

    def scratch(self, trials, span):
        bf16, f32, dma = jnp.bfloat16, jnp.float32, pltpu.SemaphoreType.DMA
        return [
            pltpu.VMEM((self.padded, LANES), bf16),
            pltpu.VMEM((self.group, self.piece_rows, LANES), bf16),
            pltpu.VMEM((trials, self.piece_rows, LANES), bf16),
            pltpu.VMEM((trials, self.piece_rows, LANES), bf16),
            pltpu.VMEM((trials, self.piece_rows, LANES), bf16),
            pltpu.VMEM((self.padded, LANES), bf16),
            pltpu.VMEM((self.padded, LANES), f32),
            pltpu.VMEM((2 * self.windows * self.blocks, span), bf16),
            dma((self.hubs,)),
            dma((self.group,)),
            dma((2,)),
            dma((self.group,)),
            dma((self.hubs,)),
        ]

    def bind(self, refs, trials, width, trial, me):
        (
            self.stored,
            self.candidates,
            self.chosen,
            self.across,
            self.settled,
            self.gathered,
            self.widened,
            self.blocked,
            self.piece_send,
            self.piece_recv,
            self.swap_sem,
            self.chosen_send,
            self.chosen_recv,
        ) = refs
        self.trials, self.width, self.trial, self.me = trials, width, trial, me
        self.my_group = me // self.group
        self.local = lax.rem(me, self.group)
        back = pow(SPREAD, -1, self.group)
        turn = lax.rem(self.local * back + self.group - self.first_hub, self.group)
        self.is_hub = turn < self.hubs
        self.my_hub = jnp.minimum(turn, self.hubs - 1)
        self.my_rows = self.piece(self.my_hub)

    def hub_local(self, hub):
        return lax.rem((hub + self.first_hub) * SPREAD, self.group)

    def piece(self, hub):
        return pl.ds(pl.multiple_of(hub * self.piece_rows, TILE), self.piece_rows)

    def place(self, flat):
        return (lax.rem(flat, self.trials), flat // self.trials)

    def near(self, local):
        return self.place(self.my_group * self.group + local)

    def lay_out(self, held):
        for window in range(self.windows):
            for number in range(self.channel_rows):
                rows = pl.ds(window * self.window_rows + number, 2, stride=self.channel_rows)
                lanes = pl.ds(number * LANES, LANES)
                self.widened[rows, :] = held[window, :, lanes].astype(jnp.float32)
        rest = self.padded - self.rows
        if rest:
            self.widened[pl.ds(self.rows, rest), :] = jnp.zeros((rest, LANES), jnp.float32)
        self.stored[...] = self.widened[...].astype(jnp.bfloat16)

    def piece_copy(self, hub):
        return pltpu.make_async_remote_copy(
            src_ref=self.stored.at[self.piece(hub)],
            dst_ref=self.candidates.at[self.local],
            send_sem=self.piece_send.at[hub],
            recv_sem=self.piece_recv.at[self.local],
            device_id=self.near(self.hub_local(hub)),
            device_id_type=MESH,
        )

    def each_other_hub(self, act):
        @pl.loop(0, self.hubs)
        def _(step):
            hub = lax.rem(self.local + step, self.hubs)

            @pl.when(self.hub_local(hub) != self.local)
            def _():
                act(hub)

    def each_other_device(self, act):
        @pl.loop(1, self.group)
        def _(step):
            act(lax.rem(self.local + step, self.group))

    def scatter(self):
        self.each_other_hub(lambda hub: self.piece_copy(hub).start())

        @pl.when(self.is_hub)
        def _():
            self.candidates[self.local] = self.stored[self.my_rows, :]

    def chosen_copy(self, target):
        return pltpu.make_async_remote_copy(
            src_ref=self.settled.at[lax.rem(target, self.trials)],
            dst_ref=self.gathered.at[self.my_rows],
            send_sem=self.chosen_send.at[target],
            recv_sem=self.chosen_recv.at[self.my_hub],
            device_id=self.near(target),
            device_id_type=MESH,
        )

    def arrival(self, ref, send_sem, recv_sem, device):
        return pltpu.make_async_remote_copy(
            src_ref=ref,
            dst_ref=ref,
            send_sem=send_sem,
            recv_sem=recv_sem,
            device_id=self.near(device),
            device_id_type=MESH,
        )

    def by_window(self, take):
        number = lax.broadcasted_iota(jnp.int32, (self.piece_rows, LANES), 0)
        number = number + self.my_hub * self.piece_rows
        kept = take(0)
        for window in range(1, self.windows):
            kept = jnp.where(number >= window * self.window_rows, take(window), kept)
        return kept.astype(jnp.bfloat16)

    def flat_owner(self, owners_ref, window, which):
        owner = owners_ref[window, which]
        return lax.rem(owner, self.width) * self.trials + owner // self.width

    def swap_copy(self):
        return pltpu.make_async_remote_copy(
            src_ref=self.chosen,
            dst_ref=self.across,
            send_sem=self.swap_sem.at[0],
            recv_sem=self.swap_sem.at[1],
            device_id=self.place(lax.rem(self.me + self.group, 2 * self.group)),
            device_id_type=MESH,
        )

    def choose(self, owners_ref):
        @pl.when(self.is_hub)
        def _():
            self.each_other_device(
                lambda other: self.arrival(
                    self.candidates.at[other],
                    self.piece_send.at[0],
                    self.piece_recv.at[other],
                    other,
                ).wait_recv()
            )
            for which in range(self.trials):

                def take(window):
                    source = lax.rem(self.flat_owner(owners_ref, window, which), self.group)
                    return self.candidates[source].astype(jnp.float32)

                self.chosen[which] = self.by_window(take)
            self.swap_copy().start()

    def settle(self, owners_ref):
        @pl.when(self.is_hub)
        def _():
            self.swap_copy().wait()
            shape = (self.piece_rows, LANES)
            for which in range(self.trials):
                mine = self.chosen[which].astype(jnp.float32)
                theirs = self.across[which].astype(jnp.float32)

                def take(window):
                    holder = self.flat_owner(owners_ref, window, which) // self.group
                    return jnp.where(jnp.full(shape, holder) == self.my_group, mine, theirs)

                self.settled[which] = self.by_window(take)
            self.each_other_device(lambda target: self.chosen_copy(target).start())
            self.gathered[self.my_rows, :] = self.settled[self.trial]

    def collect(self, chunks):
        self.each_other_hub(
            lambda hub: self.arrival(
                self.gathered.at[self.piece(hub)],
                self.chosen_send.at[0],
                self.chosen_recv.at[hub],
                self.hub_local(hub),
            ).wait_recv()
        )
        self.widened[...] = self.gathered[...].astype(jnp.float32)
        for pair in range(2 * self.windows):
            for number in range(chunks + 1):
                begin = pair * self.channel_rows + number
                rows = pl.ds(pair * self.blocks, self.blocks)
                self.blocked[rows, pl.ds(number * LANES, LANES)] = self.widened[
                    pl.ds(begin, self.blocks), :
                ].astype(jnp.bfloat16)

    def finish(self):
        self.each_other_hub(lambda hub: self.piece_copy(hub).wait_send())

        @pl.when(self.is_hub)
        def _():
            self.each_other_device(lambda target: self.chosen_copy(target).wait_send())


def kernel(plan, *refs):
    width, trials, per, chunks, half, whole = plan
    operands, out_ref, refs = refs[:6], refs[6], refs[7:]
    locals_, refs = refs[:6], refs[6:]
    half_refs, whole_refs, refs = refs[:13], refs[13:26], refs[26:]
    owners_ref, counts_ref, partners_ref, taps_ref, spectra_ref, halved_ref = locals_
    (
        send_taps,
        recv_taps,
        flipped,
        own_toeplitz,
        partner_toeplitz,
        planes,
        doubles,
        totals,
        taps_send,
        taps_recv,
        local_sem,
    ) = refs
    windows, whole_blocks, half_blocks = whole.windows, whole.blocks, half.blocks
    trial = lax.axis_index("trial")
    column = lax.axis_index("tmpl")
    me = column * trials + trial
    half.bind(half_refs, trials, width, trial, me)
    whole.bind(whole_refs, trials, width, trial, me)

    local_copies = [
        pltpu.make_async_copy(operands[number], locals_[number], local_sem.at[number])
        for number in range(6)
    ]
    for copy in reversed(local_copies):
        copy.start()

    barrier = pltpu.get_barrier_semaphore()

    def greet(place):
        pl.semaphore_signal(barrier, inc=1, device_id=place, device_id_type=MESH)

    far_column = (1 - me // whole.group) * (width // 2)
    whole.each_other_device(lambda other: greet(whole.near(other)))

    @pl.loop(0, width // 2)
    def _(step):
        greet((trial, far_column + step))

    local_copies[5].wait()
    half.lay_out(halved_ref)
    pl.semaphore_wait(barrier, whole.group - 1 + width // 2)
    half.scatter()
    local_copies[4].wait()
    whole.lay_out(spectra_ref)
    whole.scatter()
    for copy in local_copies[:4]:
        copy.wait()

    row_number = lax.broadcasted_iota(jnp.int32, (LANES, LANES), 0)
    lane_number = lax.broadcasted_iota(jnp.int32, (LANES, LANES), 1)
    masks = [
        row_number[step * TILE : (step + 1) * TILE] >= lane_number[:TILE]
        for step in range(LANES // TILE)
    ]
    flip = ((row_number + lane_number) % LANES == 0).astype(jnp.bfloat16)
    for number in range(chunks):
        held = taps_ref[:, :, pl.ds(number * LANES, LANES)].astype(jnp.float32)
        held = held.reshape(2 * per, LANES).astype(jnp.bfloat16)
        turned = jnp.dot(held, flip, preferred_element_type=jnp.float32)
        flipped[:, pl.ds(2 * number, 2), :] = turned.reshape(per, 2, LANES)

    first = column * per

    @pl.loop(0, width)
    def _(receiver):
        slot = jnp.int32(0)
        for position in range(per):
            named = partners_ref[receiver * per + position] - first
            slot = jnp.where((named >= 0) & (named < per), named, slot)
        rows = flipped[slot]
        send_taps[receiver] = jnp.concatenate([rows, rows], axis=0).astype(jnp.bfloat16)

    def taps_copy(receiver):
        return pltpu.make_async_remote_copy(
            src_ref=send_taps.at[receiver],
            dst_ref=recv_taps.at[column],
            send_sem=taps_send.at[receiver],
            recv_sem=taps_recv.at[column],
            device_id=(trial, receiver),
            device_id_type=MESH,
        )

    @pl.loop(1, width)
    def _(step):
        taps_copy(lax.rem(column + step, width)).start()

    recv_taps[column] = send_taps[column]

    def build_own(begin, end):
        @pl.loop(begin, end, unroll=2)
        def _(slot):
            toeplitz_into(own_toeplitz, slot, flipped[slot], chunks, masks)

    build_own(0, per // 2)
    half.choose(owners_ref)
    build_own(per // 2, 3 * per // 4)
    half.settle(owners_ref)
    whole.choose(owners_ref)
    build_own(3 * per // 4, per)
    whole.settle(owners_ref)

    @pl.loop(1, width)
    def _(step):
        other = lax.rem(column + step, width)
        pltpu.make_async_remote_copy(
            src_ref=recv_taps.at[other],
            dst_ref=recv_taps.at[other],
            send_sem=taps_send.at[0],
            recv_sem=taps_recv.at[other],
            device_id=(trial, other),
            device_id_type=MESH,
        ).wait_recv()

    @pl.loop(0, per, unroll=2)
    def _(slot):
        source = jnp.maximum(partners_ref[first + slot], 0) // per
        rows = recv_taps[source].astype(jnp.float32)
        toeplitz_into(partner_toeplitz, slot, rows, chunks, masks)

    def powers_of(rows_ref, matrix, blocks):
        product = jnp.dot(rows_ref[...], matrix, preferred_element_type=jnp.float32)
        result = []
        for window in range(windows):
            real = product[2 * window * blocks : (2 * window + 1) * blocks]
            imag = product[(2 * window + 1) * blocks : (2 * window + 2) * blocks]
            re = real[:, :LANES] - imag[:, LANES:]
            im = real[:, LANES:] + imag[:, :LANES]
            result.append(re * re + im * im)
        return result

    half.collect(chunks)

    @pl.loop(0, per, unroll=4)
    def _(slot):
        values = powers_of(half.blocked, partner_toeplitz[slot], half_blocks)
        planes[slot] = jnp.concatenate(values, axis=0).astype(jnp.bfloat16)

    doubling_row = lax.broadcasted_iota(jnp.int32, (LANES, 2 * LANES), 0)
    doubling_lane = lax.broadcasted_iota(jnp.int32, (LANES, 2 * LANES), 1)
    doubling = (doubling_row == doubling_lane // 2).astype(jnp.bfloat16)

    @pl.loop(0, per, unroll=4)
    def _(slot):
        doubled = jnp.dot(planes[slot], doubling, preferred_element_type=jnp.float32)
        for window in range(windows):
            base = (window * per + slot) * whole_blocks
            part = doubled[window * half_blocks : (window + 1) * half_blocks]
            for side in range(2):
                doubles[pl.ds(base + side, half_blocks, stride=2), :] = part[
                    :, side * LANES : (side + 1) * LANES
                ]

    whole.collect(chunks)
    pitch = per + 1
    live = jnp.full((whole_blocks, LANES), counts_ref[column], jnp.int32)

    @pl.loop(0, per, unroll=4)
    def _(slot):
        values = powers_of(whole.blocked, own_toeplitz[slot], whole_blocks)
        for window in range(windows):
            base = pl.multiple_of((window * per + slot) * whole_blocks, 8)
            total = values[window] + doubles[pl.ds(base, whole_blocks), :]
            rows = pl.ds(window * whole_blocks * pitch + slot, whole_blocks, stride=pitch)
            totals[rows, :] = jnp.where(live > slot, total, 0.0)

    for window in range(windows):
        for block in range(whole_blocks):
            rows = pl.ds((window * whole_blocks + block) * pitch, per)
            out_ref[window, :, pl.ds(block * LANES, LANES)] = totals[rows, :].astype(jnp.bfloat16)

    @pl.loop(1, width)
    def _(step):
        taps_copy(lax.rem(column + step, width)).wait_send()

    half.finish()
    whole.finish()


def body(spectra, half_spectra, kernels, owners, counts, partners):
    width = lax.axis_size("tmpl")
    trials = lax.axis_size("trial")
    group = width * trials // 2
    per, _, taps = kernels.shape
    windows = spectra.shape[0]
    chunks = taps // LANES
    whole_bins = spectra.shape[4] - taps
    whole_blocks = whole_bins // LANES
    half_blocks = (half_spectra.shape[4] - taps) // LANES
    half_hubs = max(1, group * (half_blocks + chunks) // (whole_blocks + half_blocks + 2 * chunks))
    half = Stream(group, windows, half_blocks, chunks, 0, half_hubs)
    whole = Stream(group, windows, whole_blocks, chunks, half.hubs, group - half.hubs)
    plan = (width, trials, per, chunks, half, whole)
    span = (chunks + 1) * LANES
    bf16, f32 = jnp.bfloat16, jnp.float32
    dma = pltpu.SemaphoreType.DMA
    operands = (owners, counts, partners, kernels, spectra[:, 0, 0], half_spectra[:, 0, 0])
    operands = tuple(pltpu.with_memory_space_constraint(held, pltpu.HBM) for held in operands)
    near = (pltpu.SMEM, pltpu.SMEM, pltpu.SMEM, pltpu.VMEM, pltpu.VMEM, pltpu.VMEM)
    hbm = pl.BlockSpec(memory_space=pltpu.HBM)
    tap_rows = -(-2 * chunks // TILE) * TILE * (2 if 2 * chunks % TILE == 0 else 1)
    flops = 4 * per * 2 * span * windows * LANES * (whole_blocks + half_blocks)
    powers = pl.pallas_call(
        functools.partial(kernel, plan),
        out_shape=jax.ShapeDtypeStruct((windows, per, whole_bins), bf16),
        in_specs=[hbm] * 6,
        out_specs=pl.BlockSpec(memory_space=pltpu.VMEM),
        scratch_shapes=[
            *[space(held.shape, held.dtype) for space, held in zip(near, operands)],
            *half.scratch(trials, span),
            *whole.scratch(trials, span),
            pltpu.VMEM((width, tap_rows, LANES), bf16),
            pltpu.VMEM((width, tap_rows, LANES), bf16),
            pltpu.VMEM((per, 2 * chunks, LANES), f32),
            pltpu.VMEM((per, span, 2 * LANES), bf16),
            pltpu.VMEM((per, span, 2 * LANES), bf16),
            pltpu.VMEM((per, windows * half_blocks, LANES), bf16),
            pltpu.VMEM((windows * per * whole_blocks, LANES), f32),
            pltpu.VMEM((windows * whole_blocks * (per + 1), LANES), f32),
            dma((width,)),
            dma((width,)),
            dma((6,)),
        ],
        compiler_params=pltpu.CompilerParams(
            collective_id=0, has_side_effects=True, vmem_limit_bytes=48 * 1024 * 1024
        ),
        cost_estimate=pl.CostEstimate(flops=flops, bytes_accessed=2 * windows * per * whole_bins, transcendentals=0),
    )(*operands)
    return powers[:, None]


def solution(mesh):
    return jax.shard_map(
        body,
        mesh=mesh,
        in_specs=(
            P(None, "trial", "tmpl", None, None),
            P(None, "trial", "tmpl", None, None),
            P("tmpl", None, None),
            P(),
            P(),
            P(),
        ),
        out_specs=P(None, "trial", "tmpl", None),
        check_vma=False,
    )
```

```python
import functools

import jax
import jax.numpy as jnp
from jax import lax
from jax.experimental import pallas as pl
from jax.experimental.pallas import tpu as pltpu
from jax.sharding import PartitionSpec as P

LANES = 128
TILE = 16
MESH = pl.DeviceIdType.MESH


def toeplitz_into(target, slot, chunk_rows, chunks, masks):
    zero = jnp.zeros((TILE, LANES), jnp.bfloat16)
    steps = LANES // TILE
    for part in range(2):
        previous = [zero] * steps
        for number in range(chunks + 1):
            current = [zero] * steps
            if number < chunks:
                row = 2 * number + part
                spread = jnp.broadcast_to(chunk_rows[row : row + 1], (TILE, LANES))
                turned = pltpu.roll(spread, 0, 1, stride=1, stride_axis=0).astype(jnp.bfloat16)
                current = [turned] + [
                    pltpu.roll(turned, step * TILE, 1) for step in range(1, steps)
                ]
            for step in range(steps):
                block = jnp.where(masks[step], current[step], previous[step])
                rows = pl.ds(number * LANES + step * TILE, TILE)
                target[slot, rows, pl.ds(part * LANES, LANES)] = block
            previous = current


SPREAD = 5


class Stream:
    def __init__(self, group, windows, blocks, chunks, first_hub, most_hubs):
        self.group, self.windows, self.blocks, self.first_hub = group, windows, blocks, first_hub
        self.channel_rows = blocks + chunks
        self.window_rows = 2 * self.channel_rows
        self.rows = windows * self.window_rows
        tiles = -(-self.rows // TILE)
        piece_tiles = -(-tiles // most_hubs)
        self.hubs = -(-tiles // piece_tiles)
        self.piece_rows = piece_tiles * TILE
        self.padded = self.hubs * self.piece_rows

    def scratch(self, trials, span):
        bf16, f32, dma = jnp.bfloat16, jnp.float32, pltpu.SemaphoreType.DMA
        return [
            pltpu.VMEM((self.padded, LANES), bf16),
            pltpu.VMEM((self.group, self.piece_rows, LANES), bf16),
            pltpu.VMEM((trials, self.piece_rows, LANES), bf16),
            pltpu.VMEM((trials, self.piece_rows, LANES), bf16),
            pltpu.VMEM((trials, self.piece_rows, LANES), bf16),
            pltpu.VMEM((self.padded, LANES), bf16),
            pltpu.VMEM((self.padded, LANES), f32),
            pltpu.VMEM((2 * self.windows * self.blocks, span), bf16),
            dma((self.hubs,)),
            dma((self.group,)),
            dma((2,)),
            dma((self.group,)),
            dma((self.hubs,)),
        ]

    def bind(self, refs, trials, width, trial, me):
        (
            self.stored,
            self.candidates,
            self.chosen,
            self.across,
            self.settled,
            self.gathered,
            self.widened,
            self.blocked,
            self.piece_send,
            self.piece_recv,
            self.swap_sem,
            self.chosen_send,
            self.chosen_recv,
        ) = refs
        self.trials, self.width, self.trial, self.me = trials, width, trial, me
        self.my_group = me // self.group
        self.local = lax.rem(me, self.group)
        back = pow(SPREAD, -1, self.group)
        turn = lax.rem(self.local * back + self.group - self.first_hub, self.group)
        self.is_hub = turn < self.hubs
        self.my_hub = jnp.minimum(turn, self.hubs - 1)
        self.my_rows = self.piece(self.my_hub)

    def hub_local(self, hub):
        return lax.rem((hub + self.first_hub) * SPREAD, self.group)

    def piece(self, hub):
        return pl.ds(pl.multiple_of(hub * self.piece_rows, TILE), self.piece_rows)

    def place(self, flat):
        return (lax.rem(flat, self.trials), flat // self.trials)

    def near(self, local):
        return self.place(self.my_group * self.group + local)

    def lay_out(self, held):
        for window in range(self.windows):
            for number in range(self.channel_rows):
                rows = pl.ds(window * self.window_rows + number, 2, stride=self.channel_rows)
                lanes = pl.ds(number * LANES, LANES)
                self.widened[rows, :] = held[window, :, lanes].astype(jnp.float32)
        rest = self.padded - self.rows
        if rest:
            self.widened[pl.ds(self.rows, rest), :] = jnp.zeros((rest, LANES), jnp.float32)
        self.stored[...] = self.widened[...].astype(jnp.bfloat16)

    def piece_copy(self, hub):
        return pltpu.make_async_remote_copy(
            src_ref=self.stored.at[self.piece(hub)],
            dst_ref=self.candidates.at[self.local],
            send_sem=self.piece_send.at[hub],
            recv_sem=self.piece_recv.at[self.local],
            device_id=self.near(self.hub_local(hub)),
            device_id_type=MESH,
        )

    def each_other_hub(self, act):
        @pl.loop(0, self.hubs)
        def _(step):
            hub = lax.rem(self.local + step, self.hubs)

            @pl.when(self.hub_local(hub) != self.local)
            def _():
                act(hub)

    def each_other_device(self, act):
        @pl.loop(1, self.group)
        def _(step):
            act(lax.rem(self.local + step, self.group))

    def scatter(self):
        self.each_other_hub(lambda hub: self.piece_copy(hub).start())

        @pl.when(self.is_hub)
        def _():
            self.candidates[self.local] = self.stored[self.my_rows, :]

    def chosen_copy(self, target):
        return pltpu.make_async_remote_copy(
            src_ref=self.settled.at[lax.rem(target, self.trials)],
            dst_ref=self.gathered.at[self.my_rows],
            send_sem=self.chosen_send.at[target],
            recv_sem=self.chosen_recv.at[self.my_hub],
            device_id=self.near(target),
            device_id_type=MESH,
        )

    def arrival(self, ref, send_sem, recv_sem, device):
        return pltpu.make_async_remote_copy(
            src_ref=ref,
            dst_ref=ref,
            send_sem=send_sem,
            recv_sem=recv_sem,
            device_id=self.near(device),
            device_id_type=MESH,
        )

    def by_window(self, take):
        number = lax.broadcasted_iota(jnp.int32, (self.piece_rows, LANES), 0)
        number = number + self.my_hub * self.piece_rows
        kept = take(0)
        for window in range(1, self.windows):
            kept = jnp.where(number >= window * self.window_rows, take(window), kept)
        return kept.astype(jnp.bfloat16)

    def flat_owner(self, owners_ref, window, which):
        owner = owners_ref[window, which]
        return lax.rem(owner, self.width) * self.trials + owner // self.width

    def swap_copy(self):
        return pltpu.make_async_remote_copy(
            src_ref=self.chosen,
            dst_ref=self.across,
            send_sem=self.swap_sem.at[0],
            recv_sem=self.swap_sem.at[1],
            device_id=self.place(lax.rem(self.me + self.group, 2 * self.group)),
            device_id_type=MESH,
        )

    def choose(self, owners_ref):
        @pl.when(self.is_hub)
        def _():
            self.each_other_device(
                lambda other: self.arrival(
                    self.candidates.at[other],
                    self.piece_send.at[0],
                    self.piece_recv.at[other],
                    other,
                ).wait_recv()
            )
            for which in range(self.trials):

                def take(window):
                    source = lax.rem(self.flat_owner(owners_ref, window, which), self.group)
                    return self.candidates[source].astype(jnp.float32)

                self.chosen[which] = self.by_window(take)
            self.swap_copy().start()

    def settle(self, owners_ref):
        @pl.when(self.is_hub)
        def _():
            self.swap_copy().wait()
            shape = (self.piece_rows, LANES)
            for which in range(self.trials):
                mine = self.chosen[which].astype(jnp.float32)
                theirs = self.across[which].astype(jnp.float32)

                def take(window):
                    holder = self.flat_owner(owners_ref, window, which) // self.group
                    return jnp.where(jnp.full(shape, holder) == self.my_group, mine, theirs)

                self.settled[which] = self.by_window(take)
            self.each_other_device(lambda target: self.chosen_copy(target).start())
            self.gathered[self.my_rows, :] = self.settled[self.trial]

    def collect(self, chunks):
        self.each_other_hub(
            lambda hub: self.arrival(
                self.gathered.at[self.piece(hub)],
                self.chosen_send.at[0],
                self.chosen_recv.at[hub],
                self.hub_local(hub),
            ).wait_recv()
        )
        self.widened[...] = self.gathered[...].astype(jnp.float32)
        for pair in range(2 * self.windows):
            for number in range(chunks + 1):
                begin = pair * self.channel_rows + number
                rows = pl.ds(pair * self.blocks, self.blocks)
                self.blocked[rows, pl.ds(number * LANES, LANES)] = self.widened[
                    pl.ds(begin, self.blocks), :
                ].astype(jnp.bfloat16)

    def finish(self):
        self.each_other_hub(lambda hub: self.piece_copy(hub).wait_send())

        @pl.when(self.is_hub)
        def _():
            self.each_other_device(lambda target: self.chosen_copy(target).wait_send())


def kernel(plan, *refs):
    width, trials, per, chunks, half, whole = plan
    operands, out_ref, refs = refs[:6], refs[6], refs[7:]
    locals_, refs = refs[:6], refs[6:]
    half_refs, whole_refs, refs = refs[:13], refs[13:26], refs[26:]
    owners_ref, counts_ref, partners_ref, taps_ref, spectra_ref, halved_ref = locals_
    (
        send_taps,
        recv_taps,
        flipped,
        own_toeplitz,
        partner_toeplitz,
        planes,
        doubles,
        totals,
        taps_send,
        taps_recv,
        local_sem,
    ) = refs
    windows, whole_blocks, half_blocks = whole.windows, whole.blocks, half.blocks
    trial = lax.axis_index("trial")
    column = lax.axis_index("tmpl")
    me = column * trials + trial
    half.bind(half_refs, trials, width, trial, me)
    whole.bind(whole_refs, trials, width, trial, me)

    local_copies = [
        pltpu.make_async_copy(operands[number], locals_[number], local_sem.at[number])
        for number in range(6)
    ]
    for copy in reversed(local_copies):
        copy.start()

    barrier = pltpu.get_barrier_semaphore()

    def greet(place):
        pl.semaphore_signal(barrier, inc=1, device_id=place, device_id_type=MESH)

    far_column = (1 - me // whole.group) * (width // 2)
    whole.each_other_device(lambda other: greet(whole.near(other)))

    @pl.loop(0, width // 2)
    def _(step):
        greet((trial, far_column + step))

    local_copies[5].wait()
    half.lay_out(halved_ref)
    pl.semaphore_wait(barrier, whole.group - 1 + width // 2)
    half.scatter()
    local_copies[4].wait()
    whole.lay_out(spectra_ref)
    whole.scatter()
    for copy in local_copies[:4]:
        copy.wait()

    row_number = lax.broadcasted_iota(jnp.int32, (LANES, LANES), 0)
    lane_number = lax.broadcasted_iota(jnp.int32, (LANES, LANES), 1)
    masks = [
        row_number[step * TILE : (step + 1) * TILE] >= lane_number[:TILE]
        for step in range(LANES // TILE)
    ]
    flip = ((row_number + lane_number) % LANES == 0).astype(jnp.bfloat16)
    for number in range(chunks):
        held = taps_ref[:, :, pl.ds(number * LANES, LANES)].astype(jnp.float32)
        held = held.reshape(2 * per, LANES).astype(jnp.bfloat16)
        turned = jnp.dot(held, flip, preferred_element_type=jnp.float32)
        flipped[:, pl.ds(2 * number, 2), :] = turned.reshape(per, 2, LANES)

    first = column * per

    @pl.loop(0, width)
    def _(receiver):
        slot = jnp.int32(0)
        for position in range(per):
            named = partners_ref[receiver * per + position] - first
            slot = jnp.where((named >= 0) & (named < per), named, slot)
        rows = flipped[slot]
        send_taps[receiver] = jnp.concatenate([rows, rows], axis=0).astype(jnp.bfloat16)

    def taps_copy(receiver):
        return pltpu.make_async_remote_copy(
            src_ref=send_taps.at[receiver],
            dst_ref=recv_taps.at[column],
            send_sem=taps_send.at[receiver],
            recv_sem=taps_recv.at[column],
            device_id=(trial, receiver),
            device_id_type=MESH,
        )

    @pl.loop(1, width)
    def _(step):
        taps_copy(lax.rem(column + step, width)).start()

    recv_taps[column] = send_taps[column]

    def build_own(begin, end):
        @pl.loop(begin, end, unroll=2)
        def _(slot):
            toeplitz_into(own_toeplitz, slot, flipped[slot], chunks, masks)

    build_own(0, per // 2)
    half.choose(owners_ref)
    build_own(per // 2, 3 * per // 4)
    half.settle(owners_ref)
    whole.choose(owners_ref)
    build_own(3 * per // 4, per)
    whole.settle(owners_ref)

    @pl.loop(1, width)
    def _(step):
        other = lax.rem(column + step, width)
        pltpu.make_async_remote_copy(
            src_ref=recv_taps.at[other],
            dst_ref=recv_taps.at[other],
            send_sem=taps_send.at[0],
            recv_sem=taps_recv.at[other],
            device_id=(trial, other),
            device_id_type=MESH,
        ).wait_recv()

    @pl.loop(0, per, unroll=2)
    def _(slot):
        source = jnp.maximum(partners_ref[first + slot], 0) // per
        rows = recv_taps[source].astype(jnp.float32)
        toeplitz_into(partner_toeplitz, slot, rows, chunks, masks)

    def powers_of(rows_ref, matrix, blocks):
        product = jnp.dot(rows_ref[...], matrix, preferred_element_type=jnp.float32)
        result = []
        for window in range(windows):
            real = product[2 * window * blocks : (2 * window + 1) * blocks]
            imag = product[(2 * window + 1) * blocks : (2 * window + 2) * blocks]
            re = real[:, :LANES] - imag[:, LANES:]
            im = real[:, LANES:] + imag[:, :LANES]
            result.append(re * re + im * im)
        return result

    half.collect(chunks)

    @pl.loop(0, per, unroll=8)
    def _(slot):
        values = powers_of(half.blocked, partner_toeplitz[slot], half_blocks)
        planes[slot] = jnp.concatenate(values, axis=0).astype(jnp.bfloat16)

    doubling_row = lax.broadcasted_iota(jnp.int32, (LANES, 2 * LANES), 0)
    doubling_lane = lax.broadcasted_iota(jnp.int32, (LANES, 2 * LANES), 1)
    doubling = (doubling_row == doubling_lane // 2).astype(jnp.bfloat16)

    @pl.loop(0, per, unroll=8)
    def _(slot):
        doubled = jnp.dot(planes[slot], doubling, preferred_element_type=jnp.float32)
        for window in range(windows):
            base = (window * per + slot) * whole_blocks
            part = doubled[window * half_blocks : (window + 1) * half_blocks]
            for side in range(2):
                doubles[pl.ds(base + side, half_blocks, stride=2), :] = part[
                    :, side * LANES : (side + 1) * LANES
                ]

    whole.collect(chunks)
    pitch = per + 1
    live = jnp.full((whole_blocks, LANES), counts_ref[column], jnp.int32)

    @pl.loop(0, per, unroll=8)
    def _(slot):
        values = powers_of(whole.blocked, own_toeplitz[slot], whole_blocks)
        for window in range(windows):
            base = pl.multiple_of((window * per + slot) * whole_blocks, 8)
            total = values[window] + doubles[pl.ds(base, whole_blocks), :]
            rows = pl.ds(window * whole_blocks * pitch + slot, whole_blocks, stride=pitch)
            totals[rows, :] = jnp.where(live > slot, total, 0.0)

    for window in range(windows):
        for block in range(whole_blocks):
            rows = pl.ds((window * whole_blocks + block) * pitch, per)
            out_ref[window, :, pl.ds(block * LANES, LANES)] = totals[rows, :].astype(jnp.bfloat16)

    @pl.loop(1, width)
    def _(step):
        taps_copy(lax.rem(column + step, width)).wait_send()

    half.finish()
    whole.finish()


def body(spectra, half_spectra, kernels, owners, counts, partners):
    width = lax.axis_size("tmpl")
    trials = lax.axis_size("trial")
    group = width * trials // 2
    per, _, taps = kernels.shape
    windows = spectra.shape[0]
    chunks = taps // LANES
    whole_bins = spectra.shape[4] - taps
    whole_blocks = whole_bins // LANES
    half_blocks = (half_spectra.shape[4] - taps) // LANES
    half_hubs = max(1, group * (half_blocks + chunks) // (whole_blocks + half_blocks + 2 * chunks))
    half = Stream(group, windows, half_blocks, chunks, 0, half_hubs)
    whole = Stream(group, windows, whole_blocks, chunks, half.hubs, group - half.hubs)
    plan = (width, trials, per, chunks, half, whole)
    span = (chunks + 1) * LANES
    bf16, f32 = jnp.bfloat16, jnp.float32
    dma = pltpu.SemaphoreType.DMA
    operands = (owners, counts, partners, kernels, spectra[:, 0, 0], half_spectra[:, 0, 0])
    operands = tuple(pltpu.with_memory_space_constraint(held, pltpu.HBM) for held in operands)
    near = (pltpu.SMEM, pltpu.SMEM, pltpu.SMEM, pltpu.VMEM, pltpu.VMEM, pltpu.VMEM)
    hbm = pl.BlockSpec(memory_space=pltpu.HBM)
    tap_rows = -(-2 * chunks // TILE) * TILE * (2 if 2 * chunks % TILE == 0 else 1)
    flops = 4 * per * 2 * span * windows * LANES * (whole_blocks + half_blocks)
    powers = pl.pallas_call(
        functools.partial(kernel, plan),
        out_shape=jax.ShapeDtypeStruct((windows, per, whole_bins), bf16),
        in_specs=[hbm] * 6,
        out_specs=pl.BlockSpec(memory_space=pltpu.VMEM),
        scratch_shapes=[
            *[space(held.shape, held.dtype) for space, held in zip(near, operands)],
            *half.scratch(trials, span),
            *whole.scratch(trials, span),
            pltpu.VMEM((width, tap_rows, LANES), bf16),
            pltpu.VMEM((width, tap_rows, LANES), bf16),
            pltpu.VMEM((per, 2 * chunks, LANES), f32),
            pltpu.VMEM((per, span, 2 * LANES), bf16),
            pltpu.VMEM((per, span, 2 * LANES), bf16),
            pltpu.VMEM((per, windows * half_blocks, LANES), bf16),
            pltpu.VMEM((windows * per * whole_blocks, LANES), f32),
            pltpu.VMEM((windows * whole_blocks * (per + 1), LANES), f32),
            dma((width,)),
            dma((width,)),
            dma((6,)),
        ],
        compiler_params=pltpu.CompilerParams(
            collective_id=0, has_side_effects=True, vmem_limit_bytes=48 * 1024 * 1024
        ),
        cost_estimate=pl.CostEstimate(flops=flops, bytes_accessed=2 * windows * per * whole_bins, transcendentals=0),
    )(*operands)
    return powers[:, None]


def solution(mesh):
    return jax.shard_map(
        body,
        mesh=mesh,
        in_specs=(
            P(None, "trial", "tmpl", None, None),
            P(None, "trial", "tmpl", None, None),
            P("tmpl", None, None),
            P(),
            P(),
            P(),
        ),
        out_specs=P(None, "trial", "tmpl", None),
        check_vma=False,
    )
```
